256 devices in a mesh: dp: 64 (over z, y, core), fsdp: 4 (over x).
Axes of the slice: x: 4, y: 4, z: 8, core: 2. Of those that a mesh axis runs over, the one named last changes fastest.
Arguments:
- inputs: bfloat16 [16384, 3072], P('dp', 'fsdp'), may hold values from -6 to 6
- out_grads: bfloat16 [16384, 3072], P('dp'), may hold values from -6 to 6
- error: bfloat16 [64, 3072, 3072], P('dp', 'fsdp'), may hold values from -0.29882812 to 0.29882812
- weight: float32 [4, 768, 3072], P('fsdp', 'dp'), may hold values from -0.109375 to 0.109375
- velocity: float32 [4, 768, 3072], P('fsdp', 'dp'), may hold values from -0.03 to 0.03
- bias: float32 [3072], replicated, may hold values from -0.3 to 0.3
- bias_velocity: float32 [3072], replicated, may hold values from -1.2 to 1.2
- start_factor: bfloat16 [3072, 64], replicated, may hold values from -6 to 6
- flags: int32 [25], replicated, may hold values from 0 to 1, as said below
Outputs:
- error_new: bfloat16 [64, 3072, 3072], P('dp', 'fsdp')
- weight_new: float32 [4, 768, 3072], P('fsdp', 'dp')
- velocity_new: float32 [4, 768, 3072], P('fsdp', 'dp')
- bias_new: float32 [3072], replicated
- bias_velocity_new: float32 [3072], replicated
- factor_new: bfloat16 [3072, 64], replicated
- next_out: bfloat16 [16384, 3072], P(('dp', 'fsdp'))
The draws below stay inside these ranges and needn't reach their ends.
Inputs may be any that keep to these rules, and one draw needn't show every extreme that they name: Every entry is 0 or 1; flags[24] differs from flags[0].
All inputs are finite; a program needn't handle non-finite values.
Results may differ from the reference program's by a relative error of at most 0.0048.
Values may be sent and summed in bfloat16 or wider, within the bound.
A program may use at most 128 MiB of HBM per device.

```python
import jax
import jax.numpy as jnp
from jax import lax

D = 3072
DOUT = 3072
HEAD = 128
GROUPS = 24
RANK = 64
TOK_REP = 256
TOKENS = 16384
N_DP = 64
N_FSDP = 4


def draw_flags(key, part):
    key = jax.random.fold_in(key, 7)
    values = jax.random.randint(key, (GROUPS + 1,), 0, 2).astype(jnp.int32)
    return values.at[GROUPS].set(1 - values[0])


def block_scale(rng, extent, split, smallest, largest):
    def one(position, parts):
        steps = jax.random.uniform(jax.random.fold_in(jax.random.fold_in(rng, 6), position), (parts,), jnp.float32, smallest / len(split), largest / len(split))
        return jnp.repeat(jnp.exp(steps), extent[position] // parts).reshape((-1,) + (1,) * (len(extent) - position - 1))

    level = one(*split[0])
    for cut in split[1:]:
        level = level * one(*cut)
    return level


def normal_values(stream_key, extent, scale, bound, pieces=(), kind=jnp.bfloat16):
    gain = block_scale(stream_key, extent, pieces, -0.22, 0.18) if pieces else 1.0
    array = jax.random.normal(stream_key, extent, jnp.float32) * scale * gain
    return jnp.minimum(jnp.maximum(array, -bound), bound).astype(kind)


def setup_inputs(seed: int = 0) -> dict:
    keys = jax.random.split(jax.random.key(seed), 10)
    return {
        "inputs": normal_values(keys[0], (TOKENS, D), 1.0, 6.0, ((0, 64), (1, 4))),
        "out_grads": normal_values(keys[1], (TOKENS, DOUT), 1.0, 6.0, ((0, 64),)),
        "error": normal_values(keys[2], (N_DP, D, DOUT), 0.05, 0.29882812, ((0, 64), (1, 4))),
        "weight": normal_values(keys[3], (N_FSDP, D // N_FSDP, DOUT), D ** -0.5, 0.109375, ((0, 4), (1, 64)), jnp.float32),
        "velocity": normal_values(keys[4], (N_FSDP, D // N_FSDP, DOUT), 0.005, 0.03, ((0, 4), (1, 64)), jnp.float32),
        "bias": normal_values(keys[5], (DOUT,), 0.05, 0.3, (), jnp.float32),
        "bias_velocity": normal_values(keys[6], (DOUT,), 0.2, 1.2, (), jnp.float32),
        "start_factor": normal_values(keys[7], (DOUT, RANK), 1.0, 6.0),
        "flags": draw_flags(jax.random.fold_in(keys[9], 71), 0),
    }


trust_coef = 0.02
decay_coef = 0.0001
momentum_coef = 0.9
learn_rate = 4.0

def reference(inputs, out_grads, error, weight, velocity, bias, bias_velocity, start_factor, flags):
    highest = lax.Precision.HIGHEST
    factor_in = start_factor.astype(jnp.float32)
    inputs_rep = inputs.reshape(N_DP, TOK_REP, D)
    grads_rep = out_grads.reshape(N_DP, TOK_REP, DOUT)

    def power_term(packed):
        tokens_in, grads_in, error_in = packed
        projected = jnp.dot(grads_in.astype(jnp.float32), factor_in, precision=highest)
        first = jnp.dot(tokens_in.astype(jnp.float32).T, projected, precision=highest) / TOK_REP
        return first + jnp.dot(error_in.astype(jnp.float32), factor_in, precision=highest)
    power = lax.optimization_barrier(jnp.sum(lax.map(power_term, (inputs_rep, grads_rep, error)), axis=0))
    gram_matrix = jnp.dot(power.T, power, precision=highest)
    lower_factor = jnp.linalg.cholesky(gram_matrix)
    basis = jax.scipy.linalg.solve_triangular(lower_factor, power.T, lower=True).T

    def back_term(packed):
        tokens_in, grads_in, error_in = packed
        projected = jnp.dot(tokens_in.astype(jnp.float32), basis, precision=highest)
        first = jnp.dot(grads_in.astype(jnp.float32).T, projected, precision=highest) / TOK_REP
        return first + jnp.dot(error_in.astype(jnp.float32).T, basis, precision=highest)
    factor = lax.optimization_barrier(jnp.sum(lax.map(back_term, (inputs_rep, grads_rep, error)), axis=0)) / N_DP
    approx = jnp.dot(basis, factor.T, precision=highest)

    def error_term(packed):
        tokens_in, grads_in, error_in = packed
        local_grad = lax.dot_general(tokens_in.astype(jnp.float32), grads_in.astype(jnp.float32), (((0,), (0,)), ((), ())), preferred_element_type=jnp.float32) / TOK_REP
        return (local_grad + error_in.astype(jnp.float32) - approx).astype(jnp.bfloat16)
    error_new = lax.map(error_term, (inputs_rep, grads_rep, error))
    groups = DOUT // HEAD
    weight_full = weight.reshape(D, DOUT)
    velocity_full = velocity.reshape(D, DOUT)
    weight_norm = jnp.sqrt(lax.optimization_barrier(jnp.sum((weight_full * weight_full).reshape(D, groups, HEAD), axis=(0, 2))))
    grad_norm = jnp.sqrt(lax.optimization_barrier(jnp.sum((approx * approx).reshape(D, groups, HEAD), axis=(0, 2))))
    skip_weight = flags[:groups] == 1
    weight_rate = jnp.where(skip_weight, 1.0, trust_coef * weight_norm / (grad_norm + decay_coef * weight_norm))
    weight_decay = jnp.where(skip_weight, 0.0, decay_coef)
    rate_cols = jnp.broadcast_to(weight_rate[:, None], (groups, HEAD)).reshape(DOUT)
    decay_cols = jnp.broadcast_to(weight_decay[:, None], (groups, HEAD)).reshape(DOUT)
    velocity_new = momentum_coef * velocity_full + learn_rate * rate_cols * (approx + decay_cols * weight_full)
    weight_new = weight_full - velocity_new
    bias_grad = lax.optimization_barrier(jnp.sum(out_grads, axis=0, dtype=jnp.float32)) / TOKENS
    bias_norm = jnp.sqrt(jnp.sum(bias * bias))
    bias_grad_norm = jnp.sqrt(jnp.sum(bias_grad * bias_grad))
    skip_bias = flags[groups] == 1
    bias_rate = jnp.where(skip_bias, 1.0, trust_coef * bias_norm / (bias_grad_norm + decay_coef * bias_norm))
    bias_decay = jnp.where(skip_bias, 0.0, decay_coef)
    bias_velocity_new = momentum_coef * bias_velocity + learn_rate * bias_rate * (bias_grad + bias_decay * bias)
    bias_new = bias - bias_velocity_new
    projected_out = jnp.dot(inputs.astype(jnp.float32), weight_new.astype(jnp.bfloat16).astype(jnp.float32), preferred_element_type=jnp.float32)
    next_out = (projected_out + bias_new).astype(jnp.bfloat16)
    return (error_new, weight_new.reshape(N_FSDP, D // N_FSDP, DOUT), velocity_new.reshape(N_FSDP, D // N_FSDP, DOUT), bias_new, bias_velocity_new, factor.astype(jnp.bfloat16), next_out)
```

```python
import jax
import jax.numpy as jnp
from jax import lax
from jax.experimental import pallas as pl
from jax.experimental.pallas import tpu as pltpu
from jax.sharding import PartitionSpec as P

HEAD = 128
MESH = pl.DeviceIdType.MESH

trust_coef = 0.02
decay_coef = 0.0001
momentum_coef = 0.9
learn_rate = 4.0

NX, NY, NZ, NC = 4, 4, 8, 2
RANK = 64
FEAT = 768
COLS = 3072
PW = FEAT + 128
HALF = COLS // 2
QUART = HALF // 4
CB = FEAT // NC


def nt(a, b):
    return lax.dot_general(a, b, (((1,), (1,)), ((), ())), preferred_element_type=jnp.float32)


def nn(a, b):
    return lax.dot_general(a, b, (((1,), (0,)), ((), ())), preferred_element_type=jnp.float32)


def pieces(a):
    hi = a.astype(jnp.bfloat16)
    lo = (a - hi.astype(jnp.float32)).astype(jnp.bfloat16)
    return jnp.concatenate([hi, lo], axis=0)


def fold(a):
    n = a.shape[0] // 2
    return a[:n] + a[n:]


def cholesky_inverse(gram):
    n = gram.shape[0]
    rows = lax.broadcasted_iota(jnp.int32, (n, 2 * n), 0)
    cols = lax.broadcasted_iota(jnp.int32, (n, 2 * n), 1)
    eye = jnp.where(cols - n == rows, 1.0, 0.0).astype(jnp.float32)
    work = jnp.concatenate([gram, eye[:, n:]], axis=1)
    first = lax.broadcasted_iota(jnp.int32, (n, 1), 0)
    for k in range(n):
        pivot = work[k : k + 1, k : k + 1]
        inv = lax.rsqrt(pivot)
        inv = inv * (1.5 - 0.5 * pivot * inv * inv)
        row = work[k : k + 1, :] * inv
        col = jnp.where(first > k, work[:, k : k + 1] * inv, 0.0)
        work = jnp.where(rows == k, row, work - col * row)
    return work[:, n:]


def step_kernel(
    x_ref, g_ref, e_ref, st_ref, extra_ref, w_ref, v_ref,
    qt_ref, pt_ref, sums_ref, xp_ref, yu_ref, yw_ref,
    ppart, precv, pz, pfull, gsend, gx,
    zpart, zc, zsum, z1, z1s, z2, zz, z3, zfull,
    wv, wrecv, stage, wbuf, xall, wh, wt, ya, yb, ys, yr, ysw, yrw,
    send_sem, recv_sem,
):
    f32, bf16 = jnp.float32, jnp.bfloat16
    dp = lax.axis_index("dp")
    x = lax.axis_index("fsdp")
    z, y, c = dp // (NY * NC), (dp // NC) % NY, dp % NC
    yc = y * NC + c

    def at_yc(k):
        return (z * NY * NC + k, x)

    def at_z(k):
        return (k * NY * NC + yc, x)

    def at_x(k):
        return (dp, k)

    def at_y(k):
        return (z * NY * NC + k * NC + c, x)

    def at_xc(k, core):
        return (z * NY * NC + y * NC + core, k)

    yc_peers = [lax.rem(yc + k, NY * NC) for k in range(1, NY * NC)]
    z_peers = [lax.rem(z + k, NZ) for k in range(1, NZ)]
    x_peers = [lax.rem(x + k, NX) for k in range(1, NX)]
    y_peers = [lax.rem(y + k, NY) for k in range(1, NY)]
    xc_peers = [(x, 1 - c)] + [(k, core) for k in x_peers for core in (c, 1 - c)]
    other = at_xc(x, 1 - c)

    barrier = pltpu.get_barrier_semaphore()
    greet = [at_yc(k) for k in yc_peers] + [at_z(k) for k in z_peers]
    greet += [at_xc(k, core) for k in x_peers for core in (c, 1 - c)]
    for d in greet:
        pl.semaphore_signal(barrier, inc=1, device_id=d, device_id_type=MESH)

    count = [0]
    sent = []

    def send(src, dst, device):
        i = count[0]
        count[0] += 1
        copy = pltpu.make_async_remote_copy(
            src_ref=src, dst_ref=dst, send_sem=send_sem.at[i], recv_sem=recv_sem.at[i],
            device_id=device, device_id_type=MESH,
        )
        copy.start()
        sent.append(copy)
        return copy

    def arrive(copies):
        for copy in copies:
            copy.wait_recv()

    own = w_ref.shape[0]
    wv[0:own] = w_ref[...]
    wv[own : 2 * own] = v_ref[...]
    xall[c, x] = x_ref[...]
    pl.semaphore_wait(barrier, len(greet))

    def cols_of(k, core):
        return wv.at[:, pl.ds(pl.multiple_of(k * FEAT + core * CB, 128), CB)]

    wv_copies = [send(cols_of(k, core), wrecv.at[x, c], at_xc(k, core)) for k, core in xc_peers]
    x_copies = [send(x_ref, xall.at[c, x], at_x(k)) for k in x_peers]
    wrecv[x, c] = wv[:, pl.ds(pl.multiple_of(x * FEAT + c * CB, 128), CB)]

    st = st_ref[...]
    gst = nt(st, g_ref[...])
    pt = fold(nn(pieces(gst), x_ref[...])) * (1.0 / x_ref.shape[0]) + nt(st, e_ref[...])
    extra = extra_ref[...]
    for k in range(NY * NC):
        ppart[k, :, 0:FEAT] = pt[8 * k : 8 * k + 8]
        ppart[k, :, FEAT:PW] = extra
    copies = [send(ppart.at[k], precv.at[yc], at_yc(k)) for k in yc_peers]
    precv[yc] = ppart[yc]

    def first_half(iz):
        return wbuf.at[iz, :, pl.ds(0, 2)]

    def ring(chunk, held, step):
        out = []
        if step < NZ // 2:
            piece = chunk(lax.rem(z - step + NZ, NZ))
            out.append(send(piece, piece, at_z(lax.rem(z + 1, NZ))))
        if step < NZ // 2 - 1:
            piece = chunk(lax.rem(z + step, NZ))
            out.append(send(piece, piece, at_z(lax.rem(z + NZ - 1, NZ))))
        return out

    def small(iz):
        return wbuf.at[iz, y, pl.ds(2, 2)]

    def pack():
        arrive(wv_copies)
        for k in range(NX):
            first, second = wrecv[k, 0], wrecv[k, 1]
            stage[0, 0:own] = first[0:own]
            stage[0, own : 2 * own] = second[0:own]
            stage[1, 0:own] = first[own : 2 * own]
            stage[1, own : 2 * own] = second[own : 2 * own]
            full = stage[0]
            high = full.astype(bf16).astype(f32)
            rest = full - high - momentum_coef * stage[1]
            wbuf[z, y, k] = jnp.concatenate([high, rest], axis=0).astype(bf16)
        piece = wbuf.at[z, y, pl.ds(0, 2)]
        return [send(piece, piece, at_y(k)) for k in y_peers], ring(small, None, 0)

    def column(iy, ix, n):
        return wbuf.at[:, iy, pl.ds(ix, n)]

    def deinterleave(k):
        for iz in range(NZ):
            for iy in range(0, NY, 2):
                u0 = wbuf[iz, iy, k].astype(f32)
                u1 = wbuf[iz, iy + 1, k].astype(f32)
                row = iz * 96 + iy * 24
                wh[row : row + 48] = jnp.concatenate([u0[0:24], u1[0:24]], axis=0).astype(bf16)
                wt[row : row + 48] = jnp.concatenate([u0[24:48], u1[24:48]], axis=0).astype(bf16)

    def products(k, first):
        deinterleave(k)
        for core in range(NC):
            a = nn(xall[core, k], wh[...])
            b = nn(xall[core, k], wt[...])
            ya[core] = a if first else ya[core] + a
            yb[core] = b if first else yb[core] + b

    a_copies, b_copies = pack()

    arrive(copies)
    total = precv[0]
    for k in range(1, NY * NC):
        total = total + precv[k]
    pz[z] = total
    copies = [send(pz.at[z], pz.at[z], at_z(k)) for k in z_peers]
    arrive(b_copies)
    b_copies = ring(small, None, 1)
    arrive(a_copies)
    a_copies = ring(first_half, None, 0)
    arrive(copies)
    total = pz[0]
    for k in range(1, NZ):
        total = total + pz[k]
    pfull[yc] = total
    copies = [send(pfull.at[yc], pfull.at[yc], at_yc(k)) for k in yc_peers]
    arrive(b_copies)
    b_copies = ring(small, None, 2)
    arrive(copies)

    ptot = pfull[...].reshape(RANK, PW)
    pt = ptot[:, 0:FEAT]
    pp = pieces(pt)
    xpt = fold(nt(pp, x_ref[...]))
    gram = lax.dot_general(
        pt, pt, (((1,), (1,)), ((), ())), precision=lax.Precision.HIGHEST,
        preferred_element_type=f32,
    )
    for k in range(NX):
        gsend[k, 0:RANK, 0:RANK] = gram
        gsend[k, 0:RANK, RANK:] = xpt[:, k * 64 : (k + 1) * 64]
        gsend[k, RANK:, :] = ptot[0:8, FEAT:]
    gram_copies = [send(gsend.at[k], gx.at[x], at_x(k)) for k in x_peers]
    gx[x] = gsend[x]
    arrive(b_copies)
    b_copies = ring(small, None, 3)

    zpart[...] = fold(nn(pieces(xpt), g_ref[...])) * (1.0 / x_ref.shape[0]) + fold(nn(pp, e_ref[...]))

    core_copy = send(zpart.at[pl.ds(pl.multiple_of((1 - c) * 32, 8), 32)], zc, other)
    arrive(b_copies)
    b_copies = [send(column(y, 2, 2), column(y, 2, 2), at_y(lax.rem(y + k, NY))) for k in (1, NY - 1)]
    arrive(x_copies)
    x_core = send(xall.at[c], xall.at[c], other)
    arrive([core_copy])
    mine = zpart[pl.ds(pl.multiple_of(c * 32, 8), 32)] + zc[...]
    for k in range(4):
        zsum[0, k] = mine[8 * k : 8 * k + 8, :HALF]
        zsum[1, k] = mine[8 * k : 8 * k + 8, HALF:]
    axes = (((y, y_peers, at_y), (x, x_peers, at_x)), ((x, x_peers, at_x), (y, y_peers, at_y)))
    copies = []
    for h in range(2):
        me, peers, at = axes[h][0]
        copies += [send(zsum.at[h, k], z1.at[h, me], at(k)) for k in peers]
        z1[h, me] = zsum[h, me]
    arrive(a_copies)
    a_copies = ring(first_half, None, 1)
    arrive(copies)
    copies = []
    for h in range(2):
        me, peers, at = axes[h][1]
        total = z1[h, 0] + z1[h, 1] + z1[h, 2] + z1[h, 3]
        for k in range(4):
            z1s[h, k] = total[:, k * QUART : (k + 1) * QUART]
        copies += [send(z1s.at[h, k], z2.at[h, me], at(k)) for k in peers]
        z2[h, me] = z1s[h, me]
    arrive(copies)
    for h in range(2):
        zz[z, h] = z2[h, 0] + z2[h, 1] + z2[h, 2] + z2[h, 3]
    copies = [send(zz.at[z], zz.at[z], at_z(k)) for k in z_peers]
    arrive(a_copies)
    a_copies = ring(first_half, None, 2)

    arrive(gram_copies)
    both = gx[0, 0:RANK] + gx[1, 0:RANK] + gx[2, 0:RANK] + gx[3, 0:RANK]
    for k in range(NX):
        sums_ref[k] = gx[k, RANK:, :]
    inverse = cholesky_inverse(both[:, 0:RANK])
    highest = lax.Precision.HIGHEST
    pt_ref[...] = jnp.dot(inverse, pt, precision=highest, preferred_element_type=f32)
    xp_ref[...] = jnp.dot(inverse, both, precision=highest, preferred_element_type=f32)

    arrive(copies)
    total = zz[0]
    for k in range(1, NZ):
        total = total + zz[k]
    copies = []
    for h in range(2):
        me, peers, at = axes[h][1]
        z3[h, me] = total[h]
        copies += [send(z3.at[h, me], z3.at[h, me], at(k)) for k in peers]
    arrive(b_copies)
    b_copies = [
        send(column(lax.rem(y + 1, NY), 2, 1), column(lax.rem(y + 1, NY), 2, 1), at_y(lax.rem(y + NY - 1, NY))),
        send(column(lax.rem(y + NY - 1, NY), 3, 1), column(lax.rem(y + NY - 1, NY), 3, 1), at_y(lax.rem(y + 1, NY))),
    ]
    arrive(copies)
    copies = []
    for h in range(2):
        me, peers, at = axes[h][0]
        for k in range(4):
            zfull[c, h, me, :, k * QUART : (k + 1) * QUART] = z3[h, k]
        copies += [send(zfull.at[c, h, me], zfull.at[c, h, me], at(k)) for k in peers]
    arrive(a_copies)
    a_copies = ring(first_half, None, 3)
    arrive(copies)
    copies = [send(zfull.at[c], zfull.at[c], other)]
    arrive([x_core])
    arrive(copies)
    for h in range(2):
        zt = jnp.concatenate([zfull[0, h].reshape(32, HALF), zfull[1, h].reshape(32, HALF)], axis=0)
        qt_ref[:, h * HALF : (h + 1) * HALF] = jnp.dot(
            inverse, zt, precision=highest, preferred_element_type=f32
        ) * (1.0 / (NC * NY * NZ))

    arrive(b_copies)
    products(2, True)
    products(3, False)
    arrive(a_copies)
    products(0, False)
    products(1, False)
    for core in range(NC):
        for k in range(NX):
            a = ya[core, k * 64 : (k + 1) * 64]
            ys[k, core] = a + yb[core, k * 64 : (k + 1) * 64]
            ysw[k, core] = a.astype(bf16)
    copies = []
    for k, core in xc_peers:
        copies.append(send(ys.at[k, core], yr.at[x, c], at_xc(k, core)))
        copies.append(send(ysw.at[k, core], yrw.at[x, c], at_xc(k, core)))
    yr[x, c] = ys[x, c]
    yrw[x, c] = ysw[x, c]
    arrive(copies)
    for k in range(NX):
        for core in range(NC):
            cols = slice(k * FEAT + core * CB, k * FEAT + core * CB + CB)
            yu_ref[:, cols] = yr[k, core]
            yw_ref[:, cols] = yrw[k, core]
    for copy in sent:
        copy.wait_send()


def step_call(x, g, e, st, extra, w, v):
    f32, bf16 = jnp.float32, jnp.bfloat16
    copies = (7 + 3) + 7 + 3 + (2 + 2 + 2 + 1) + 7 + (2 + 2 + 2 + 1) + 7 + 3 + 1 + 2 + 1 + 6 + 6 + 7 + 6 + 2 + 6 + 1 + 14
    return pl.pallas_call(
        step_kernel,
        out_shape=(
            jax.ShapeDtypeStruct((RANK, COLS), f32),
            jax.ShapeDtypeStruct((RANK, FEAT), f32),
            jax.ShapeDtypeStruct((NX, 8, 128), f32),
            jax.ShapeDtypeStruct((RANK, 128), f32),
            jax.ShapeDtypeStruct((64, COLS), f32),
            jax.ShapeDtypeStruct((64, COLS), bf16),
        ),
        in_specs=[pl.BlockSpec(memory_space=pltpu.VMEM)] * 7,
        out_specs=[pl.BlockSpec(memory_space=pltpu.VMEM)] * 6,
        scratch_shapes=[
            pltpu.VMEM((8, 8, PW), f32),
            pltpu.VMEM((8, 8, PW), f32),
            pltpu.VMEM((NZ, 8, PW), f32),
            pltpu.VMEM((8, 8, PW), f32),
            pltpu.VMEM((NX, RANK + 8, 128), f32),
            pltpu.VMEM((NX, RANK + 8, 128), f32),
            pltpu.VMEM((RANK, COLS), f32),
            pltpu.VMEM((32, COLS), f32),
            pltpu.VMEM((2, 4, 8, HALF), f32),
            pltpu.VMEM((2, 4, 8, HALF), f32),
            pltpu.VMEM((2, 4, 8, QUART), f32),
            pltpu.VMEM((2, 4, 8, QUART), f32),
            pltpu.VMEM((NZ, 2, 8, QUART), f32),
            pltpu.VMEM((2, 4, 8, QUART), f32),
            pltpu.VMEM((2, 2, 4, 8, HALF), f32),
            pltpu.VMEM((24, COLS), f32),
            pltpu.VMEM((NX, NC, 24, CB), f32),
            pltpu.VMEM((2, 24, CB), f32),
            pltpu.VMEM((NZ, NY, NX, 48, CB), bf16),
            pltpu.VMEM((NC, NX, 256, FEAT), bf16),
            pltpu.VMEM((FEAT, CB), bf16),
            pltpu.VMEM((FEAT, CB), bf16),
            pltpu.VMEM((NC, 256, CB), f32),
            pltpu.VMEM((NC, 256, CB), f32),
            pltpu.VMEM((NX, NC, 64, CB), f32),
            pltpu.VMEM((NX, NC, 64, CB), f32),
            pltpu.VMEM((NX, NC, 64, CB), bf16),
            pltpu.VMEM((NX, NC, 64, CB), bf16),
            pltpu.SemaphoreType.DMA((copies,)),
            pltpu.SemaphoreType.DMA((copies,)),
        ],
        compiler_params=pltpu.CompilerParams(
            collective_id=0, has_side_effects=True, vmem_limit_bytes=56 * 2**20
        ),
        name="step",
    )(x, g, e, st, extra, w, v)


def error_kernel(x_ref, g_ref, e_ref, pt_ref, qt_ref, out_ref, left):
    f32, bf16 = jnp.float32, jnp.bfloat16

    @pl.when(pl.program_id(0) == 0)
    def _():
        left[0:256] = (x_ref[...].astype(f32) * (1.0 / 256)).astype(bf16)
        hilo = pieces(-pt_ref[...])
        left[256:384] = hilo
        left[384:448] = hilo[0:RANK]

    q = qt_ref[...]
    hi = q.astype(bf16)
    lo = (q - hi.astype(f32)).astype(bf16)
    right = jnp.concatenate([g_ref[...], hi, hi, lo], axis=0)
    total = lax.dot_general(left[...], right, (((0,), (0,)), ((), ())), preferred_element_type=f32)
    out_ref[...] = (total + e_ref[...].astype(f32)).astype(bf16)


def error_call(x, g, e, pt, qt):
    tile = 512
    return pl.pallas_call(
        error_kernel,
        grid=(COLS // tile,),
        out_shape=jax.ShapeDtypeStruct((FEAT, COLS), jnp.bfloat16),
        in_specs=[
            pl.BlockSpec((256, FEAT), lambda i: (0, 0)),
            pl.BlockSpec((256, tile), lambda i: (0, i)),
            pl.BlockSpec((FEAT, tile), lambda i: (0, i)),
            pl.BlockSpec((RANK, FEAT), lambda i: (0, 0)),
            pl.BlockSpec((RANK, tile), lambda i: (0, i)),
        ],
        out_specs=pl.BlockSpec((FEAT, tile), lambda i: (0, i)),
        scratch_shapes=[pltpu.VMEM((448, FEAT), jnp.bfloat16)],
        compiler_params=pltpu.CompilerParams(vmem_limit_bytes=32 * 2**20),
        name="error_new",
    )(x, g, e, pt, qt)


def shards(inputs, out_grads, error, weight, velocity, bias, bias_velocity, start_factor, flags):
    highest = lax.Precision.HIGHEST
    tok_rows = inputs.shape[0]
    own_rows = weight.shape[1]
    out_cols = weight.shape[2]
    groups = out_cols // HEAD
    data_count = lax.axis_size("dp")
    data_index = lax.axis_index("dp")
    feat_index = lax.axis_index("fsdp")

    weight_local = weight[0]
    grad_cols = lax.dynamic_slice_in_dim(out_grads, feat_index * FEAT, FEAT, 1)
    bias_local = jnp.sum(grad_cols, axis=0, dtype=jnp.float32).reshape(FEAT // 128, 128)
    weight_square = jnp.sum((weight_local * weight_local).reshape(own_rows, groups, HEAD), axis=(0, 2))
    extra = jnp.concatenate(
        [bias_local, jnp.pad(weight_square, (0, 128 - groups))[None], jnp.zeros((1, 128), jnp.float32)], axis=0
    )
    qt, pt, sums, xp, yu, yw = step_call(
        inputs, out_grads, error[0], start_factor.T, extra, weight_local, velocity[0]
    )
    error_new = error_call(inputs, out_grads, error[0], pt, qt)[None]
    bias_total = sums[:, 0:6, :].reshape(out_cols)
    weight_total = jnp.sum(sums[:, 6, :groups], axis=0)

    basis_own = lax.dynamic_slice_in_dim(pt, data_index * own_rows, own_rows, 1)
    left = jnp.concatenate([basis_own, xp[:, 64:128]], axis=1)
    both = lax.dot_general(left, qt, (((0,), (0,)), ((), ())), precision=highest)
    grad_own, token_part = both[:own_rows], both[own_rows:]
    grad_total = jnp.sum(jnp.sum(qt * qt, axis=0).reshape(groups, HEAD), axis=1)

    weight_norm = jnp.sqrt(weight_total)
    grad_norm = jnp.sqrt(grad_total)
    skip_weight = flags[:groups] == 1
    weight_rate = jnp.where(
        skip_weight, 1.0, trust_coef * weight_norm / (grad_norm + decay_coef * weight_norm)
    )
    weight_decay = jnp.where(skip_weight, 0.0, decay_coef)
    rate_cols = jnp.broadcast_to(weight_rate[:, None], (groups, HEAD)).reshape(out_cols)
    decay_cols = jnp.broadcast_to(weight_decay[:, None], (groups, HEAD)).reshape(out_cols)
    velocity_new = momentum_coef * velocity[0] + learn_rate * rate_cols * (
        grad_own + decay_cols * weight_local
    )
    weight_new = weight_local - velocity_new
    bias_grad = bias_total / (tok_rows * data_count)
    bias_norm = jnp.sqrt(jnp.sum(bias * bias))
    bias_grad_norm = jnp.sqrt(jnp.sum(bias_grad * bias_grad))
    skip_bias = flags[groups] == 1
    bias_rate = jnp.where(
        skip_bias, 1.0, trust_coef * bias_norm / (bias_grad_norm + decay_coef * bias_norm)
    )
    bias_decay = jnp.where(skip_bias, 0.0, decay_coef)
    bias_velocity_new = momentum_coef * bias_velocity + learn_rate * bias_rate * (
        bias_grad + bias_decay * bias
    )
    bias_new = bias - bias_velocity_new
    next_out = (
        yu - learn_rate * rate_cols * (token_part + decay_cols * yw.astype(jnp.float32)) + bias_new
    ).astype(jnp.bfloat16)
    return (
        error_new,
        weight_new[None],
        velocity_new[None],
        bias_new,
        bias_velocity_new,
        qt.T.astype(jnp.bfloat16),
        next_out,
    )


def solution(mesh):
    in_specs = (
        P("dp", "fsdp"),
        P("dp", None),
        P("dp", "fsdp", None),
        P("fsdp", "dp", None),
        P("fsdp", "dp", None),
        P(),
        P(),
        P(),
        P(),
    )
    out_specs = (
        P("dp", "fsdp", None),
        P("fsdp", "dp", None),
        P("fsdp", "dp", None),
        P(),
        P(),
        P(),
        P(("dp", "fsdp"), None),
    )
    return jax.shard_map(shards, mesh=mesh, in_specs=in_specs, out_specs=out_specs, check_vma=False)
```

```python
import jax
import jax.numpy as jnp
from jax import lax
from jax.experimental import pallas as pl
from jax.experimental.pallas import tpu as pltpu
from jax.sharding import PartitionSpec as P

HEAD = 128
MESH = pl.DeviceIdType.MESH

trust_coef = 0.02
decay_coef = 0.0001
momentum_coef = 0.9
learn_rate = 4.0

NX, NY, NZ, NC = 4, 4, 8, 2
RANK = 64
FEAT = 768
COLS = 3072
PW = FEAT + 128
HALF = COLS // 2
QUART = HALF // 4
CB = FEAT // NC
LOADS = 3
TILE = 512


def nt(a, b):
    return lax.dot_general(a, b, (((1,), (1,)), ((), ())), preferred_element_type=jnp.float32)


def nn(a, b):
    return lax.dot_general(a, b, (((1,), (0,)), ((), ())), preferred_element_type=jnp.float32)


def pieces(a):
    hi = a.astype(jnp.bfloat16)
    lo = (a - hi.astype(jnp.float32)).astype(jnp.bfloat16)
    return jnp.concatenate([hi, lo], axis=0)


def fold(a):
    n = a.shape[0] // 2
    return a[:n] + a[n:]


def eliminate(work, start, stop):
    n = work.shape[0]
    rows = lax.broadcasted_iota(jnp.int32, (n, 2 * n), 0)
    first = lax.broadcasted_iota(jnp.int32, (n, 1), 0)
    for k in range(start, stop):
        pivot = work[k : k + 1, k : k + 1]
        inv = lax.rsqrt(pivot)
        inv = inv * (1.5 - 0.5 * pivot * inv * inv)
        row = work[k : k + 1, :] * inv
        col = jnp.where(first > k, work[:, k : k + 1] * inv, 0.0)
        work = jnp.where(rows == k, row, work - col * row)
    return work


def beside_identity(gram):
    n = gram.shape[0]
    rows = lax.broadcasted_iota(jnp.int32, (n, n), 0)
    cols = lax.broadcasted_iota(jnp.int32, (n, n), 1)
    return jnp.concatenate([gram, jnp.where(rows == cols, 1.0, 0.0).astype(jnp.float32)], axis=1)


def step_kernel(
    x_ref, g_ref, e_hbm, s_ref, w_ref, v_ref, b_ref, bv_ref, flags_ref,
    qt_ref, left_ref, sums_ref, own_ref, out_ref,
    ppart, precv, pz, pfull, gsend, gx,
    zpart, zc, zsum, z1, z1s, z2, zz, z3, zfull,
    wv, wrecv, stage, wbuf, xall, wh, wt, ya, yb, xph, tokens, moved, osend, orecv,
    e_ref, extra, heads, load_sem, send_sem, recv_sem,
):
    f32, bf16 = jnp.float32, jnp.bfloat16
    dp = lax.axis_index("dp")
    x = lax.axis_index("fsdp")
    z, y, c = dp // (NY * NC), (dp // NC) % NY, dp % NC
    yc = y * NC + c

    def at_yc(k):
        return (z * NY * NC + k, x)

    def at_z(k):
        return (k * NY * NC + yc, x)

    def at_x(k):
        return (dp, k)

    def at_y(k):
        return (z * NY * NC + k * NC + c, x)

    def at_xc(k, core):
        return (z * NY * NC + y * NC + core, k)

    yc_peers = [lax.rem(yc + k, NY * NC) for k in range(1, NY * NC)]
    z_peers = [lax.rem(z + k, NZ) for k in range(1, NZ)]
    x_peers = [lax.rem(x + k, NX) for k in range(1, NX)]
    y_peers = [lax.rem(y + k, NY) for k in range(1, NY)]
    xc_peers = [(x, 1 - c)] + [(k, core) for k in x_peers for core in (c, 1 - c)]
    other = at_xc(x, 1 - c)

    barrier = pltpu.get_barrier_semaphore()
    greet = [at_yc(k) for k in yc_peers] + [at_z(k) for k in z_peers]
    greet += [at_xc(k, core) for k in x_peers for core in (c, 1 - c)]
    for d in greet:
        pl.semaphore_signal(barrier, inc=1, device_id=d, device_id_type=MESH)

    count = [0]
    sent = []

    def send(src, dst, device):
        i = count[0]
        count[0] += 1
        copy = pltpu.make_async_remote_copy(
            src_ref=src, dst_ref=dst, send_sem=send_sem.at[i], recv_sem=recv_sem.at[i],
            device_id=device, device_id_type=MESH,
        )
        copy.start()
        sent.append(copy)
        return copy

    def arrive(copies):
        for copy in copies:
            copy.wait_recv()

    own = w_ref.shape[0]
    rows = FEAT // LOADS
    loads = []
    for k in range(LOADS):
        block = pl.ds(k * rows, rows)
        loads.append(pltpu.make_async_copy(e_hbm.at[block], e_ref.at[block], load_sem.at[k]))
        loads[k].start()
    w = w_ref[:, 0, :]
    wv[0:own] = w
    wv[own : 2 * own] = v_ref[:, 0, :]
    xall[c, x] = x_ref[...]

    ones = jnp.ones((8, x_ref.shape[0]), bf16)
    column_sums = nn(ones, g_ref[:, pl.ds(pl.multiple_of(x * FEAT, 128), FEAT)])
    squares = jnp.sum(w * w, axis=0, keepdims=True)
    groups = COLS // HEAD
    for k in range(groups):
        heads[k : k + 1] = squares[:, k * HEAD : (k + 1) * HEAD]
    lane = lax.broadcasted_iota(jnp.int32, (groups, 128), 1)
    row = lax.broadcasted_iota(jnp.int32, (groups, 128), 0)
    norms = jnp.where(lane == row, jnp.sum(heads[...], axis=1, keepdims=True), 0.0)
    extra[...] = jnp.zeros_like(extra)
    for k in range(FEAT // 128):
        extra[k : k + 1] = column_sums[0:1, k * 128 : (k + 1) * 128]
    extra[6:7] = jnp.sum(norms, axis=0, keepdims=True)

    factor = s_ref[...].T
    gst = nn(g_ref[...], factor).T
    pt = fold(nn(pieces(gst), x_ref[...])) * (1.0 / x_ref.shape[0])
    pl.semaphore_wait(barrier, len(greet))

    def cols_of(k, core):
        return wv.at[:, pl.ds(pl.multiple_of(k * FEAT + core * CB, 128), CB)]

    wv_copies = [send(cols_of(k, core), wrecv.at[x, c], at_xc(k, core)) for k, core in xc_peers]
    wrecv[x, c] = wv[:, pl.ds(pl.multiple_of(x * FEAT + c * CB, 128), CB)]

    for k in range(LOADS):
        loads[k].wait()
        cols = slice(k * rows, (k + 1) * rows)
        part = pt[:, cols] + nn(e_ref[cols], factor).T
        for i in range(NY * NC):
            ppart[i, :, cols] = part[8 * i : 8 * i + 8]
    for i in range(NY * NC):
        ppart[i, :, FEAT:PW] = extra[...]
    copies = [send(ppart.at[k], precv.at[yc], at_yc(k)) for k in yc_peers]
    precv[yc] = ppart[yc]

    def first_half(iz, part, n):
        return wbuf.at[iz, :, pl.ds(part, n)]

    def small(iz, part, n):
        return wbuf.at[iz, y, pl.ds(2 + part, n)]

    def ring(chunk, step):
        last = step == NZ // 2 - 1
        up = chunk(lax.rem(z - step + NZ, NZ), 0, 1 if last else 2)
        down = chunk(lax.rem(z + step, NZ), 1 if last else 0, 1 if last else 2)
        return [send(up, up, at_z(lax.rem(z + 1, NZ))), send(down, down, at_z(lax.rem(z + NZ - 1, NZ)))]

    def pack():
        arrive(wv_copies)
        for k in range(NX):
            first, second = wrecv[k, 0], wrecv[k, 1]
            stage[0, 0:own] = first[0:own]
            stage[0, own : 2 * own] = second[0:own]
            stage[1, 0:own] = first[own : 2 * own]
            stage[1, own : 2 * own] = second[own : 2 * own]
            full = stage[0]
            high = full.astype(bf16).astype(f32)
            rest = full - high - momentum_coef * stage[1]
            wbuf[z, y, k] = jnp.concatenate([high, rest], axis=0).astype(bf16)
        piece = wbuf.at[z, y, pl.ds(0, 2)]
        return [send(piece, piece, at_y(k)) for k in y_peers], ring(small, 0)

    def column(iy, ix, n):
        return wbuf.at[:, iy, pl.ds(ix, n)]

    def deinterleave(k):
        for iz in range(NZ):
            for iy in range(0, NY, 2):
                u0 = wbuf[iz, iy, k].astype(f32)
                u1 = wbuf[iz, iy + 1, k].astype(f32)
                row = iz * 96 + iy * 24
                wh[row : row + 48] = jnp.concatenate([u0[0:24], u1[0:24]], axis=0).astype(bf16)
                wt[row : row + 48] = jnp.concatenate([u0[24:48], u1[24:48]], axis=0).astype(bf16)

    def products(k, first):
        deinterleave(k)
        for core in range(NC):
            a = nn(xall[core, k], wh[...])
            b = nn(xall[core, k], wt[...])
            ya[core] = a if first else ya[core] + a
            yb[core] = b if first else yb[core] + b

    a_copies, b_copies = pack()
    left_ref[:, 0:256] = (x_ref[...].astype(f32) * (1.0 / 256)).T.astype(bf16)

    arrive(copies)
    total = precv[0]
    for k in range(1, NY * NC):
        total = total + precv[k]
    pz[z] = total
    copies = [send(pz.at[z], pz.at[z], at_z(k)) for k in z_peers]
    arrive(b_copies)
    b_copies = ring(small, 1)
    arrive(a_copies)
    a_copies = ring(first_half, 0)
    x_copies = [send(x_ref, xall.at[c, x], at_x(k)) for k in x_peers]
    arrive(copies)
    total = pz[0]
    for k in range(1, NZ):
        total = total + pz[k]
    pfull[yc] = total
    copies = [send(pfull.at[yc], pfull.at[yc], at_yc(k)) for k in yc_peers]
    arrive(b_copies)
    b_copies = ring(small, 2)
    arrive(copies)

    ptot = pfull[...].reshape(RANK, PW)
    pt = ptot[:, 0:FEAT]
    pp = pieces(pt)
    xpt = fold(nt(pp, x_ref[...]))
    gram = lax.dot_general(
        pt, pt, (((1,), (1,)), ((), ())), precision=lax.Precision.HIGHEST,
        preferred_element_type=f32,
    )
    for k in range(NX):
        gsend[k, 0:RANK, 0:RANK] = gram
        gsend[k, 0:RANK, RANK:] = xpt[:, k * 64 : (k + 1) * 64]
        gsend[k, RANK:, :] = ptot[0:8, FEAT:]
    gram_copies = [send(gsend.at[k], gx.at[x], at_x(k)) for k in x_peers]
    gx[x] = gsend[x]
    arrive(b_copies)
    b_copies = ring(small, 3)
    arrive(a_copies)
    a_copies = ring(first_half, 1)

    zpart[...] = fold(nn(pieces(xpt), g_ref[...])) * (1.0 / x_ref.shape[0]) + fold(nn(pp, e_ref[...]))

    core_copy = send(zpart.at[pl.ds(pl.multiple_of((1 - c) * 32, 8), 32)], zc, other)
    arrive(b_copies)
    b_copies = [send(column(y, 2, 2), column(y, 2, 2), at_y(lax.rem(y + k, NY))) for k in (1, NY - 1)]
    arrive([core_copy])
    mine = zpart[pl.ds(pl.multiple_of(c * 32, 8), 32)] + zc[...]
    for k in range(4):
        zsum[0, k] = mine[8 * k : 8 * k + 8, :HALF]
        zsum[1, k] = mine[8 * k : 8 * k + 8, HALF:]
    axes = (((y, y_peers, at_y), (x, x_peers, at_x)), ((x, x_peers, at_x), (y, y_peers, at_y)))
    copies = []
    for h in range(2):
        me, peers, at = axes[h][0]
        copies += [send(zsum.at[h, k], z1.at[h, me], at(k)) for k in peers]
        z1[h, me] = zsum[h, me]
    arrive(a_copies)
    a_copies = ring(first_half, 2)
    arrive(copies)
    copies = []
    for h in range(2):
        me, peers, at = axes[h][1]
        total = z1[h, 0] + z1[h, 1] + z1[h, 2] + z1[h, 3]
        for k in range(4):
            z1s[h, k] = total[:, k * QUART : (k + 1) * QUART]
        copies += [send(z1s.at[h, k], z2.at[h, me], at(k)) for k in peers]
        z2[h, me] = z1s[h, me]
    arrive(copies)
    for h in range(2):
        zz[z, h] = z2[h, 0] + z2[h, 1] + z2[h, 2] + z2[h, 3]
    copies = [send(zz.at[z], zz.at[z], at_z(k)) for k in z_peers]
    arrive(gram_copies)
    both = gx[0, 0:RANK] + gx[1, 0:RANK] + gx[2, 0:RANK] + gx[3, 0:RANK]
    for k in range(NX):
        sums_ref[k] = gx[k, RANK:, :]
    work = eliminate(beside_identity(both[:, 0:RANK]), 0, RANK // 2)
    arrive(a_copies)
    a_copies = ring(first_half, 3)
    inverse = eliminate(work, RANK // 2, RANK)[:, RANK:]
    highest = lax.Precision.HIGHEST
    hat = jnp.dot(inverse, pt, precision=highest, preferred_element_type=f32)
    high = hat.astype(bf16).astype(f32)
    left_ref[:, 256:512] = jnp.concatenate([-high, high - hat, -high, jnp.zeros_like(hat)], axis=0).T.astype(bf16)
    feature = lax.broadcasted_iota(jnp.int32, (FEAT, 128), 0)
    wanted = lax.broadcasted_iota(jnp.int32, (FEAT, 128), 1)
    pick = jnp.where((feature == dp * own + wanted) & (wanted < own), 1.0, 0.0).astype(f32)
    own_ref[...] = jnp.dot(hat, pick, precision=highest, preferred_element_type=f32)
    xph[x, c] = jnp.dot(inverse, both, precision=highest, preferred_element_type=f32)
    token_copies = [send(xph.at[x, c], xph.at[x, c], at_xc(k, core)) for k, core in xc_peers]

    b, bv = b_ref[...], bv_ref[...]
    nb = jnp.sqrt(jnp.sum(b * b, keepdims=True))
    ng = jnp.zeros((1, 1), f32)
    for k in range(NX):
        gb = sums_ref[k, 0:6, :] * (1.0 / (256 * 64))
        ng = ng + jnp.sum(gb * gb, keepdims=True)
    ng = jnp.sqrt(ng)
    lane = lax.broadcasted_iota(jnp.int32, (1, flags_ref.shape[1]), 1)

    def skips(index):
        return jnp.sum(jnp.where(lane == index, flags_ref[...], 0), keepdims=True) == 1

    rb = jnp.where(skips(groups), 1.0, trust_coef * nb / (ng + decay_coef * nb))
    db = jnp.where(skips(groups), 0.0, decay_coef)
    biases = []
    for j in range(CB // HEAD):
        cols = pl.ds(pl.multiple_of(x * FEAT + c * CB + j * HEAD, HEAD), HEAD)
        gb = sums_ref[x, pl.ds(c * (CB // HEAD) + j, 1), :] * (1.0 / (256 * 64))
        biases.append(b_ref[:, cols] - momentum_coef * bv_ref[:, cols] - learn_rate * rb * (gb + db * b_ref[:, cols]))

    arrive(x_copies)
    x_core = send(xall.at[c], xall.at[c], other)

    arrive(copies)
    total = zz[0]
    for k in range(1, NZ):
        total = total + zz[k]
    copies = []
    for h in range(2):
        me, peers, at = axes[h][1]
        z3[h, me] = total[h]
        copies += [send(z3.at[h, me], z3.at[h, me], at(k)) for k in peers]
    arrive(b_copies)
    b_copies = [
        send(column(lax.rem(y + 1, NY), 2, 1), column(lax.rem(y + 1, NY), 2, 1), at_y(lax.rem(y + NY - 1, NY))),
        send(column(lax.rem(y + NY - 1, NY), 3, 1), column(lax.rem(y + NY - 1, NY), 3, 1), at_y(lax.rem(y + 1, NY))),
    ]
    arrive(copies)
    copies = []
    for h in range(2):
        me, peers, at = axes[h][0]
        for k in range(4):
            zfull[c, h, me, :, k * QUART : (k + 1) * QUART] = z3[h, k]
        copies += [send(zfull.at[c, h, me], zfull.at[c, h, me], at(k)) for k in peers]
    arrive([x_core])
    arrive(a_copies)
    products(0, True)
    arrive(copies)
    copies = [send(zfull.at[c], zfull.at[c], other)]
    products(1, False)
    arrive(token_copies)
    for core in range(NC):
        for k in range(NX):
            part = xph[k, core].T[64:128]
            high = part.astype(bf16).astype(f32)
            tokens[core, k * 64 : (k + 1) * 64] = jnp.concatenate(
                [high, part - high, high, jnp.zeros_like(part)], axis=1
            ).astype(bf16)
    arrive(copies)
    for h in range(2):
        zt = jnp.concatenate([zfull[0, h].reshape(32, HALF), zfull[1, h].reshape(32, HALF)], axis=0)
        qt_ref[:, h * HALF : (h + 1) * HALF] = jnp.dot(
            inverse, zt, precision=highest, preferred_element_type=f32
        ) * (1.0 / (NC * NY * NZ))

    arrive(b_copies)
    products(2, False)
    products(3, False)
    qc = qt_ref[:, pl.ds(pl.multiple_of(x * FEAT + c * CB, 128), CB)]
    qh = qc.astype(bf16)
    ql = (qc - qh.astype(f32)).astype(bf16)
    right = jnp.concatenate([qh, qh, ql, jnp.zeros_like(qh)], axis=0)
    norms = sums_ref[0, 6:7] + sums_ref[1, 6:7] + sums_ref[2, 6:7] + sums_ref[3, 6:7]
    lanes = lax.broadcasted_iota(jnp.int32, (1, 128), 1)
    rates, decays = [], []
    for j in range(CB // HEAD):
        head = x * (FEAT // HEAD) + c * (CB // HEAD) + j
        part = qc[:, j * HEAD : (j + 1) * HEAD]
        nw = jnp.sqrt(jnp.sum(jnp.where(lanes == head, norms, 0.0), keepdims=True))
        na = jnp.sqrt(jnp.sum(part * part, keepdims=True))
        skip = skips(head)
        rates.append(learn_rate * jnp.where(skip, 1.0, trust_coef * nw / (na + decay_coef * nw)))
        decays.append(jnp.where(skip, 0.0, decay_coef))
    out_copies = []
    for core in range(NC):
        moved[...] = nn(tokens[core], right)
        for j in range(CB // HEAD):
            cols = slice(j * HEAD, (j + 1) * HEAD)
            a = ya[core, :, cols]
            value = a + yb[core, :, cols] - rates[j] * (moved[:, cols] + decays[j] * a) + biases[j]
            for k in range(NX):
                osend[k, core, :, cols] = value[k * 64 : (k + 1) * 64].astype(bf16)
    for k, core in xc_peers:
        out_copies.append(send(osend.at[k, core], orecv.at[x, c], at_xc(k, core)))
    orecv[x, c] = osend[x, c]
    arrive(out_copies)
    for k in range(NX):
        for core in range(NC):
            out_ref[:, k * FEAT + core * CB : k * FEAT + core * CB + CB] = orecv[k, core]
    for copy in sent:
        copy.wait_send()


def step_call(x, g, e, factor, w, v, b, bv, flags):
    f32, bf16 = jnp.float32, jnp.bfloat16
    copies = 128
    return pl.pallas_call(
        step_kernel,
        out_shape=(
            jax.ShapeDtypeStruct((RANK, COLS), f32),
            jax.ShapeDtypeStruct((FEAT, 512), bf16),
            jax.ShapeDtypeStruct((NX, 8, 128), f32),
            jax.ShapeDtypeStruct((RANK, 128), f32),
            jax.ShapeDtypeStruct((64, COLS), bf16),
        ),
        in_specs=[pl.BlockSpec(memory_space=pltpu.VMEM)] * 2
        + [pl.BlockSpec(memory_space=pl.ANY)]
        + [pl.BlockSpec(memory_space=pltpu.VMEM)] * 6,
        out_specs=[pl.BlockSpec(memory_space=pltpu.VMEM)] * 5,
        scratch_shapes=[
            pltpu.VMEM((8, 8, PW), f32),
            pltpu.VMEM((8, 8, PW), f32),
            pltpu.VMEM((NZ, 8, PW), f32),
            pltpu.VMEM((8, 8, PW), f32),
            pltpu.VMEM((NX, RANK + 8, 128), f32),
            pltpu.VMEM((NX, RANK + 8, 128), f32),
            pltpu.VMEM((RANK, COLS), f32),
            pltpu.VMEM((32, COLS), f32),
            pltpu.VMEM((2, 4, 8, HALF), f32),
            pltpu.VMEM((2, 4, 8, HALF), f32),
            pltpu.VMEM((2, 4, 8, QUART), f32),
            pltpu.VMEM((2, 4, 8, QUART), f32),
            pltpu.VMEM((NZ, 2, 8, QUART), f32),
            pltpu.VMEM((2, 4, 8, QUART), f32),
            pltpu.VMEM((2, 2, 4, 8, HALF), f32),
            pltpu.VMEM((24, COLS), f32),
            pltpu.VMEM((NX, NC, 24, CB), f32),
            pltpu.VMEM((2, 24, CB), f32),
            pltpu.VMEM((NZ, NY, NX, 48, CB), bf16),
            pltpu.VMEM((NC, NX, 256, FEAT), bf16),
            pltpu.VMEM((FEAT, CB), bf16),
            pltpu.VMEM((FEAT, CB), bf16),
            pltpu.VMEM((NC, 256, CB), f32),
            pltpu.VMEM((NC, 256, CB), f32),
            pltpu.VMEM((NX, NC, RANK, 128), f32),
            pltpu.VMEM((NC, 256, 256), bf16),
            pltpu.VMEM((256, CB), f32),
            pltpu.VMEM((NX, NC, 64, CB), bf16),
            pltpu.VMEM((NX, NC, 64, CB), bf16),
            pltpu.VMEM((FEAT, COLS), bf16),
            pltpu.VMEM((8, 128), f32),
            pltpu.VMEM((COLS // HEAD, 128), f32),
            pltpu.SemaphoreType.DMA((LOADS,)),
            pltpu.SemaphoreType.DMA((copies,)),
            pltpu.SemaphoreType.DMA((copies,)),
        ],
        compiler_params=pltpu.CompilerParams(
            collective_id=0, has_side_effects=True, vmem_limit_bytes=56 * 2**20
        ),
        name="step",
    )(x, g, e, factor, w, v, b, bv, flags)


def finish_kernel(
    flags_ref, left_ref, g_ref, e_ref, qt_ref, sums_ref, own_ref, w_ref, v_ref, b_ref, bv_ref,
    error_ref, weight_ref, velocity_ref, bias_ref, bias_velocity_ref, factor_ref,
):
    f32, bf16 = jnp.float32, jnp.bfloat16
    highest = lax.Precision.HIGHEST
    step = pl.program_id(0)
    groups = COLS // HEAD

    @pl.when(step == 0)
    def _():
        total = jnp.concatenate(
            [sums_ref[k, r : r + 1, :] for k in range(NX) for r in range(FEAT // 128)], axis=1
        )
        gb = total * (1.0 / (256 * 64))
        b = b_ref[...]
        nb = jnp.sqrt(jnp.sum(b * b, keepdims=True))
        ng = jnp.sqrt(jnp.sum(gb * gb, keepdims=True))
        skip = flags_ref[groups] == 1
        rb = jnp.where(skip, 1.0, trust_coef * nb / (ng + decay_coef * nb))
        db = jnp.where(skip, 0.0, decay_coef)
        bv = momentum_coef * bv_ref[...] + learn_rate * rb * (gb + db * b)
        bias_velocity_ref[...] = bv
        bias_ref[...] = b - bv

    q = qt_ref[...]
    hi = q.astype(bf16)
    lo = (q - hi.astype(f32)).astype(bf16)
    right = jnp.concatenate([g_ref[...], hi, hi, lo, jnp.zeros_like(hi)], axis=0)
    error_ref[...] = (nn(left_ref[...], right) + e_ref[...].astype(f32)).astype(bf16)
    factor_ref[...] = hi

    both = lax.dot_general(
        own_ref[...], q, (((0,), (0,)), ((), ())), precision=highest, preferred_element_type=f32
    )
    own = w_ref.shape[0]
    norms = sums_ref[0, 6:7] + sums_ref[1, 6:7] + sums_ref[2, 6:7] + sums_ref[3, 6:7]
    lane = lax.broadcasted_iota(jnp.int32, (1, 128), 1)
    per = TILE // HEAD
    for j in range(per):
        cols = slice(j * HEAD, (j + 1) * HEAD)
        head = step * per + j
        nw = jnp.sqrt(jnp.sum(jnp.where(lane == head, norms, 0.0), keepdims=True))
        na = jnp.sqrt(jnp.sum(q[:, cols] * q[:, cols], keepdims=True))
        skip = flags_ref[head] == 1
        rate = jnp.where(skip, 1.0, trust_coef * nw / (na + decay_coef * nw))
        decay = jnp.where(skip, 0.0, decay_coef)
        w = w_ref[:, 0, cols]
        v = momentum_coef * v_ref[:, 0, cols] + learn_rate * rate * (both[0:own, cols] + decay * w)
        velocity_ref[:, 0, cols] = v
        weight_ref[:, 0, cols] = w - v


def finish_call(flags, left, g, e, qt, sums, own, w, v, b, bv):
    f32, bf16 = jnp.float32, jnp.bfloat16

    def whole(a):
        return pl.BlockSpec(a.shape, lambda i: (0,) * a.ndim)

    def tiled(a):
        return pl.BlockSpec(a.shape[:-1] + (TILE,), lambda i: (0,) * (a.ndim - 1) + (i,))

    return pl.pallas_call(
        finish_kernel,
        grid=(COLS // TILE,),
        out_shape=(
            jax.ShapeDtypeStruct(e.shape, bf16),
            jax.ShapeDtypeStruct(w.shape, f32),
            jax.ShapeDtypeStruct(v.shape, f32),
            jax.ShapeDtypeStruct(b.shape, f32),
            jax.ShapeDtypeStruct(bv.shape, f32),
            jax.ShapeDtypeStruct((RANK, COLS), bf16),
        ),
        in_specs=[
            pl.BlockSpec(memory_space=pltpu.SMEM),
            whole(left), tiled(g), tiled(e), tiled(qt), whole(sums), whole(own),
            tiled(w), tiled(v), whole(b), whole(bv),
        ],
        out_specs=(
            tiled(e), tiled(w), tiled(v), whole(b), whole(bv),
            tiled(qt),
        ),
        compiler_params=pltpu.CompilerParams(vmem_limit_bytes=60 * 2**20),
        name="finish",
    )(flags, left, g, e, qt, sums, own, w, v, b, bv)


def shards(inputs, out_grads, error, weight, velocity, bias, bias_velocity, start_factor, flags):
    w, v = weight.transpose(1, 0, 2), velocity.transpose(1, 0, 2)
    b, bv = bias.reshape(1, COLS), bias_velocity.reshape(1, COLS)
    qt, left, sums, own, next_out = step_call(
        inputs, out_grads, error[0], start_factor.T, w, v, b, bv, flags.reshape(1, flags.shape[0])
    )
    error_new, weight_new, velocity_new, bias_new, bias_velocity_new, factor_new = finish_call(
        flags, left, out_grads, error[0], qt, sums, own, w, v, b, bv
    )
    return (
        error_new[None],
        weight_new.transpose(1, 0, 2),
        velocity_new.transpose(1, 0, 2),
        bias_new.reshape(COLS),
        bias_velocity_new.reshape(COLS),
        factor_new.T,
        next_out,
    )


def solution(mesh):
    in_specs = (
        P("dp", "fsdp"),
        P("dp", None),
        P("dp", "fsdp", None),
        P("fsdp", "dp", None),
        P("fsdp", "dp", None),
        P(),
        P(),
        P(),
        P(),
    )
    out_specs = (
        P("dp", "fsdp", None),
        P("fsdp", "dp", None),
        P("fsdp", "dp", None),
        P(),
        P(),
        P(),
        P(("dp", "fsdp"), None),
    )
    return jax.shard_map(shards, mesh=mesh, in_specs=in_specs, out_specs=out_specs, check_vma=False)
```

```python
import jax
import jax.numpy as jnp
from jax import lax
from jax.experimental import pallas as pl
from jax.experimental.pallas import tpu as pltpu
from jax.sharding import PartitionSpec as P

HEAD = 128
MESH = pl.DeviceIdType.MESH

trust_coef = 0.02
decay_coef = 0.0001
momentum_coef = 0.9
learn_rate = 4.0

NX, NY, NZ, NC = 4, 4, 8, 2
RANK = 64
FEAT = 768
COLS = 3072
PW = FEAT + 128
HALF = COLS // 2
QUART = HALF // 4
CB = FEAT // NC
LOADS = 3
TILE = 768


def nt(a, b):
    return lax.dot_general(a, b, (((1,), (1,)), ((), ())), preferred_element_type=jnp.float32)


def nn(a, b):
    return lax.dot_general(a, b, (((1,), (0,)), ((), ())), preferred_element_type=jnp.float32)


def pieces(a):
    hi = a.astype(jnp.bfloat16)
    lo = (a - hi.astype(jnp.float32)).astype(jnp.bfloat16)
    return jnp.concatenate([hi, lo], axis=0)


def fold(a):
    n = a.shape[0] // 2
    return a[:n] + a[n:]


def eliminate(work, start, stop):
    n = work.shape[0]
    rows = lax.broadcasted_iota(jnp.int32, (n, 2 * n), 0)
    first = lax.broadcasted_iota(jnp.int32, (n, 1), 0)
    for k in range(start, stop):
        pivot = work[k : k + 1, k : k + 1]
        inv = lax.rsqrt(pivot)
        inv = inv * (1.5 - 0.5 * pivot * inv * inv)
        row = work[k : k + 1, :] * inv
        col = jnp.where(first > k, work[:, k : k + 1] * inv, 0.0)
        work = jnp.where(rows == k, row, work - col * row)
    return work


def beside_identity(gram):
    n = gram.shape[0]
    rows = lax.broadcasted_iota(jnp.int32, (n, n), 0)
    cols = lax.broadcasted_iota(jnp.int32, (n, n), 1)
    return jnp.concatenate([gram, jnp.where(rows == cols, 1.0, 0.0).astype(jnp.float32)], axis=1)


def step_kernel(
    x_ref, g_ref, e_hbm, s_ref, w_ref, v_ref, b_ref, bv_ref, flags_ref,
    qt_ref, left_ref, sums_ref, own_ref, out_ref,
    ppart, precv, pz, pfull, gsend, gx,
    zpart, zc, zsum, z1, z1s, z2, zz, z3, zfull,
    wv, wrecv, stage, wbuf, xall, wh, wt, ya, yb, xph, tokens, moved, osend, orecv,
    e_ref, extra, heads, load_sem, send_sem, recv_sem,
):
    f32, bf16 = jnp.float32, jnp.bfloat16
    dp = lax.axis_index("dp")
    x = lax.axis_index("fsdp")
    z, y, c = dp // (NY * NC), (dp // NC) % NY, dp % NC
    yc = y * NC + c

    def at_yc(k):
        return (z * NY * NC + k, x)

    def at_z(k):
        return (k * NY * NC + yc, x)

    def at_x(k):
        return (dp, k)

    def at_y(k):
        return (z * NY * NC + k * NC + c, x)

    def at_xc(k, core):
        return (z * NY * NC + y * NC + core, k)

    yc_peers = [lax.rem(yc + k, NY * NC) for k in range(1, NY * NC)]
    z_peers = [lax.rem(z + k, NZ) for k in range(1, NZ)]
    x_peers = [lax.rem(x + k, NX) for k in range(1, NX)]
    y_peers = [lax.rem(y + k, NY) for k in range(1, NY)]
    xc_peers = [(x, 1 - c)] + [(k, core) for k in x_peers for core in (c, 1 - c)]
    other = at_xc(x, 1 - c)

    barrier = pltpu.get_barrier_semaphore()
    greet = [at_yc(k) for k in yc_peers] + [at_z(k) for k in z_peers]
    greet += [at_xc(k, core) for k in x_peers for core in (c, 1 - c)]
    for d in greet:
        pl.semaphore_signal(barrier, inc=1, device_id=d, device_id_type=MESH)

    count = [0]
    sent = []

    def send(src, dst, device):
        i = count[0]
        count[0] += 1
        copy = pltpu.make_async_remote_copy(
            src_ref=src, dst_ref=dst, send_sem=send_sem.at[i], recv_sem=recv_sem.at[i],
            device_id=device, device_id_type=MESH,
        )
        copy.start()
        sent.append(copy)
        return copy

    def arrive(copies):
        for copy in copies:
            copy.wait_recv()

    own = w_ref.shape[0]
    rows = FEAT // LOADS
    loads = []
    for k in range(LOADS):
        block = pl.ds(k * rows, rows)
        loads.append(pltpu.make_async_copy(e_hbm.at[block], e_ref.at[block], load_sem.at[k]))
        loads[k].start()
    w = w_ref[:, 0, :]
    wv[0:own] = w
    wv[own : 2 * own] = v_ref[:, 0, :]
    xall[c, x] = x_ref[...]

    ones = jnp.ones((8, x_ref.shape[0]), bf16)
    column_sums = nn(ones, g_ref[:, pl.ds(pl.multiple_of(x * FEAT, 128), FEAT)])
    squares = jnp.sum(w * w, axis=0, keepdims=True)
    groups = COLS // HEAD
    for k in range(groups):
        heads[k : k + 1] = squares[:, k * HEAD : (k + 1) * HEAD]
    lane = lax.broadcasted_iota(jnp.int32, (groups, 128), 1)
    row = lax.broadcasted_iota(jnp.int32, (groups, 128), 0)
    norms = jnp.where(lane == row, jnp.sum(heads[...], axis=1, keepdims=True), 0.0)
    extra[...] = jnp.zeros_like(extra)
    for k in range(FEAT // 128):
        extra[k : k + 1] = column_sums[0:1, k * 128 : (k + 1) * 128]
    extra[6:7] = jnp.sum(norms, axis=0, keepdims=True)

    factor = s_ref[...].T
    gst = nn(g_ref[...], factor).T
    pt = fold(nn(pieces(gst), x_ref[...])) * (1.0 / x_ref.shape[0])
    pl.semaphore_wait(barrier, len(greet))

    def cols_of(k, core):
        return wv.at[:, pl.ds(pl.multiple_of(k * FEAT + core * CB, 128), CB)]

    wv_copies = [send(cols_of(k, core), wrecv.at[x, c], at_xc(k, core)) for k, core in xc_peers]
    wrecv[x, c] = wv[:, pl.ds(pl.multiple_of(x * FEAT + c * CB, 128), CB)]

    for k in range(LOADS):
        loads[k].wait()
        cols = slice(k * rows, (k + 1) * rows)
        part = pt[:, cols] + nn(e_ref[cols], factor).T
        for i in range(NY * NC):
            ppart[i, :, cols] = part[8 * i : 8 * i + 8]
    for i in range(NY * NC):
        ppart[i, :, FEAT:PW] = extra[...]
    copies = [send(ppart.at[k], precv.at[yc], at_yc(k)) for k in yc_peers]
    precv[yc] = ppart[yc]

    def first_half(iz, part, n):
        return wbuf.at[iz, :, pl.ds(part, n)]

    def small(iz, part, n):
        return wbuf.at[iz, y, pl.ds(2 + part, n)]

    def ring(chunk, step):
        last = step == NZ // 2 - 1
        up = chunk(lax.rem(z - step + NZ, NZ), 0, 1 if last else 2)
        down = chunk(lax.rem(z + step, NZ), 1 if last else 0, 1 if last else 2)
        return [send(up, up, at_z(lax.rem(z + 1, NZ))), send(down, down, at_z(lax.rem(z + NZ - 1, NZ)))]

    def pack():
        arrive(wv_copies)
        for k in range(NX):
            first, second = wrecv[k, 0], wrecv[k, 1]
            stage[0, 0:own] = first[0:own]
            stage[0, own : 2 * own] = second[0:own]
            stage[1, 0:own] = first[own : 2 * own]
            stage[1, own : 2 * own] = second[own : 2 * own]
            full = stage[0]
            high = full.astype(bf16).astype(f32)
            rest = full - high - momentum_coef * stage[1]
            wbuf[z, y, k] = jnp.concatenate([high, rest], axis=0).astype(bf16)
        piece = wbuf.at[z, y, pl.ds(0, 2)]
        return [send(piece, piece, at_y(k)) for k in y_peers], ring(small, 0)

    def column(iy, ix, n):
        return wbuf.at[:, iy, pl.ds(ix, n)]

    def deinterleave(k):
        for iz in range(NZ):
            for iy in range(0, NY, 2):
                u0 = wbuf[iz, iy, k].astype(f32)
                u1 = wbuf[iz, iy + 1, k].astype(f32)
                row = iz * 96 + iy * 24
                wh[row : row + 48] = jnp.concatenate([u0[0:24], u1[0:24]], axis=0).astype(bf16)
                wt[row : row + 48] = jnp.concatenate([u0[24:48], u1[24:48]], axis=0).astype(bf16)

    def products(k, first):
        deinterleave(k)
        for core in range(NC):
            a = nn(xall[core, k], wh[...])
            b = nn(xall[core, k], wt[...])
            ya[core] = a if first else ya[core] + a
            yb[core] = b if first else yb[core] + b

    a_copies, b_copies = pack()

    arrive(copies)
    total = precv[0]
    for k in range(1, NY * NC):
        total = total + precv[k]
    pz[z] = total
    copies = [send(pz.at[z], pz.at[z], at_z(k)) for k in z_peers]
    arrive(b_copies)
    b_copies = ring(small, 1)
    arrive(a_copies)
    a_copies = ring(first_half, 0)
    x_copies = [send(x_ref, xall.at[c, x], at_x(k)) for k in x_peers]
    arrive(copies[:2] + copies[-2:])
    arrive(b_copies)
    b_copies = ring(small, 2)
    arrive(copies[2:-2])
    total = pz[0]
    for k in range(1, NZ):
        total = total + pz[k]
    pfull[yc] = total
    copies = [send(pfull.at[yc], pfull.at[yc], at_yc(k)) for k in yc_peers]
    arrive(b_copies)
    b_copies = ring(small, 3)
    arrive(copies[:1] + copies[-1:])
    arrive(b_copies)
    b_copies = [send(column(y, 2, 2), column(y, 2, 2), at_y(lax.rem(y + k, NY))) for k in (1, NY - 1)]
    arrive(copies[1:-1])

    ptot = pfull[...].reshape(RANK, PW)
    pt = ptot[:, 0:FEAT]
    pp = pieces(pt)
    xpt = fold(nt(pp, x_ref[...]))
    gram = lax.dot_general(
        pt, pt, (((1,), (1,)), ((), ())), precision=lax.Precision.HIGHEST,
        preferred_element_type=f32,
    )
    for k in range(NX):
        gsend[k, 0:RANK, 0:RANK] = gram
        gsend[k, 0:RANK, RANK:] = xpt[:, k * 64 : (k + 1) * 64]
        gsend[k, RANK:, :] = ptot[0:8, FEAT:]
    gram_copies = [send(gsend.at[k], gx.at[x], at_x(k)) for k in x_peers]
    gx[x] = gsend[x]
    arrive(a_copies)
    a_copies = ring(first_half, 1)

    zpart[...] = fold(nn(pieces(xpt), g_ref[...])) * (1.0 / x_ref.shape[0]) + fold(nn(pp, e_ref[...]))

    core_copy = send(zpart.at[pl.ds(pl.multiple_of((1 - c) * 32, 8), 32)], zc, other)
    arrive([core_copy])
    mine = zpart[pl.ds(pl.multiple_of(c * 32, 8), 32)] + zc[...]
    for k in range(4):
        zsum[0, k] = mine[8 * k : 8 * k + 8, :HALF]
        zsum[1, k] = mine[8 * k : 8 * k + 8, HALF:]
    axes = (((y, y_peers, at_y), (x, x_peers, at_x)), ((x, x_peers, at_x), (y, y_peers, at_y)))
    copies = []
    for h in range(2):
        me, peers, at = axes[h][0]
        copies += [send(zsum.at[h, k], z1.at[h, me], at(k)) for k in peers]
        z1[h, me] = zsum[h, me]
    arrive(a_copies)
    a_copies = ring(first_half, 2)

    arrive(gram_copies)
    both = gx[0, 0:RANK] + gx[1, 0:RANK] + gx[2, 0:RANK] + gx[3, 0:RANK]
    for k in range(NX):
        sums_ref[k] = gx[k, RANK:, :]
    work = eliminate(beside_identity(both[:, 0:RANK]), 0, 24)
    arrive(copies)
    copies = []
    for h in range(2):
        me, peers, at = axes[h][1]
        total = z1[h, 0] + z1[h, 1] + z1[h, 2] + z1[h, 3]
        for k in range(4):
            z1s[h, k] = total[:, k * QUART : (k + 1) * QUART]
        copies += [send(z1s.at[h, k], z2.at[h, me], at(k)) for k in peers]
        z2[h, me] = z1s[h, me]
    work = eliminate(work, 24, 40)
    arrive(copies)
    for h in range(2):
        zz[z, h] = z2[h, 0] + z2[h, 1] + z2[h, 2] + z2[h, 3]
    copies = [send(zz.at[z], zz.at[z], at_z(k)) for k in z_peers]
    arrive(x_copies)
    x_core = send(xall.at[c], xall.at[c], other)
    arrive(a_copies)
    a_copies = ring(first_half, 3)
    arrive(b_copies)
    b_copies = [
        send(column(lax.rem(y + 1, NY), 2, 1), column(lax.rem(y + 1, NY), 2, 1), at_y(lax.rem(y + NY - 1, NY))),
        send(column(lax.rem(y + NY - 1, NY), 3, 1), column(lax.rem(y + NY - 1, NY), 3, 1), at_y(lax.rem(y + 1, NY))),
    ]
    inverse = eliminate(work, 40, RANK)[:, RANK:]
    ih = inverse.astype(bf16)
    il = (inverse - ih.astype(f32)).astype(bf16)
    inverse3 = jnp.concatenate([ih, ih, il], axis=1)

    def times_inverse(a):
        hi = a.astype(bf16)
        lo = (a - hi.astype(f32)).astype(bf16)
        return nn(inverse3, jnp.concatenate([hi, lo, hi], axis=0))

    xph[x, c] = times_inverse(both)
    token_copies = [send(xph.at[x, c], xph.at[x, c], at_xc(k, core)) for k, core in xc_peers]
    arrive(copies)
    total = zz[0]
    for k in range(1, NZ):
        total = total + zz[k]
    copies = []
    for h in range(2):
        me, peers, at = axes[h][1]
        z3[h, me] = total[h]
        copies += [send(z3.at[h, me], z3.at[h, me], at(k)) for k in peers]

    b, bv = b_ref[...], bv_ref[...]
    nb = jnp.sqrt(jnp.sum(b * b, keepdims=True))
    ng = jnp.zeros((1, 1), f32)
    for k in range(NX):
        gb = sums_ref[k, 0:6, :] * (1.0 / (256 * 64))
        ng = ng + jnp.sum(gb * gb, keepdims=True)
    ng = jnp.sqrt(ng)
    lane = lax.broadcasted_iota(jnp.int32, (1, flags_ref.shape[1]), 1)

    def skips(index):
        return jnp.sum(jnp.where(lane == index, flags_ref[...], 0), keepdims=True) == 1

    rb = jnp.where(skips(groups), 1.0, trust_coef * nb / (ng + decay_coef * nb))
    db = jnp.where(skips(groups), 0.0, decay_coef)
    biases = []
    for j in range(CB // HEAD):
        cols = pl.ds(pl.multiple_of(x * FEAT + c * CB + j * HEAD, HEAD), HEAD)
        gb = sums_ref[x, pl.ds(c * (CB // HEAD) + j, 1), :] * (1.0 / (256 * 64))
        biases.append(b_ref[:, cols] - momentum_coef * bv_ref[:, cols] - learn_rate * rb * (gb + db * b_ref[:, cols]))

    arrive(b_copies + [x_core])
    products(2, True)
    arrive(copies)
    copies = []
    for h in range(2):
        me, peers, at = axes[h][0]
        for k in range(4):
            zfull[c, h, me, :, k * QUART : (k + 1) * QUART] = z3[h, k]
        copies += [send(zfull.at[c, h, me], zfull.at[c, h, me], at(k)) for k in peers]
    products(3, False)
    arrive(a_copies)
    products(0, False)
    arrive(copies)
    copies = [send(zfull.at[c], zfull.at[c], other)]
    products(1, False)
    arrive(token_copies)
    for core in range(NC):
        for k in range(NX):
            part = xph[k, core].T[64:128]
            high = part.astype(bf16).astype(f32)
            tokens[core, k * 64 : (k + 1) * 64] = jnp.concatenate(
                [high, part - high, high, jnp.zeros_like(part)], axis=1
            ).astype(bf16)
    arrive(copies)
    for h in range(2):
        zt = jnp.concatenate([zfull[0, h].reshape(32, HALF), zfull[1, h].reshape(32, HALF)], axis=0)
        qt_ref[:, h * HALF : (h + 1) * HALF] = times_inverse(zt) * (1.0 / (NC * NY * NZ))

    qc = qt_ref[:, pl.ds(pl.multiple_of(x * FEAT + c * CB, 128), CB)]
    qh = qc.astype(bf16)
    ql = (qc - qh.astype(f32)).astype(bf16)
    right = jnp.concatenate([qh, qh, ql, jnp.zeros_like(qh)], axis=0)
    norms = sums_ref[0, 6:7] + sums_ref[1, 6:7] + sums_ref[2, 6:7] + sums_ref[3, 6:7]
    lanes = lax.broadcasted_iota(jnp.int32, (1, 128), 1)
    rates, decays = [], []
    for j in range(CB // HEAD):
        head = x * (FEAT // HEAD) + c * (CB // HEAD) + j
        part = qc[:, j * HEAD : (j + 1) * HEAD]
        nw = jnp.sqrt(jnp.sum(jnp.where(lanes == head, norms, 0.0), keepdims=True))
        na = jnp.sqrt(jnp.sum(part * part, keepdims=True))
        skip = skips(head)
        rates.append(learn_rate * jnp.where(skip, 1.0, trust_coef * nw / (na + decay_coef * nw)))
        decays.append(jnp.where(skip, 0.0, decay_coef))
    out_copies = []
    for core in (1 - c, c):
        moved[...] = nn(tokens[core], right)
        for j in range(CB // HEAD):
            cols = slice(j * HEAD, (j + 1) * HEAD)
            a = ya[core, :, cols]
            value = a + yb[core, :, cols] - rates[j] * (moved[:, cols] + decays[j] * a) + biases[j]
            for k in range(NX):
                osend[k, core, :, cols] = value[k * 64 : (k + 1) * 64].astype(bf16)
        for k in x_peers:
            out_copies.append(send(osend.at[k, core], orecv.at[x, c], at_xc(k, core)))
    out_copies.append(send(osend.at[x, 1 - c], orecv.at[x, c], other))
    orecv[x, c] = osend[x, c]

    left_ref[:, 0:256] = (x_ref[...].astype(f32) * (1.0 / 256)).T.astype(bf16)
    hat = times_inverse(pt)
    high = hat.astype(bf16).astype(f32)
    left_ref[:, 256:512] = jnp.concatenate([-high, high - hat, -high, jnp.zeros_like(hat)], axis=0).T.astype(bf16)
    feature = lax.broadcasted_iota(jnp.int32, (FEAT, 128), 0)
    wanted = lax.broadcasted_iota(jnp.int32, (FEAT, 128), 1)
    pick = jnp.where((feature == dp * own + wanted) & (wanted < own), 1.0, 0.0).astype(f32)
    own_ref[...] = jnp.dot(hat, pick, precision=lax.Precision.HIGHEST, preferred_element_type=f32)
    arrive(out_copies)
    for k in range(NX):
        for core in range(NC):
            out_ref[:, k * FEAT + core * CB : k * FEAT + core * CB + CB] = orecv[k, core]
    for copy in sent:
        copy.wait_send()


def step_call(x, g, e, factor, w, v, b, bv, flags):
    f32, bf16 = jnp.float32, jnp.bfloat16
    copies = 128
    return pl.pallas_call(
        step_kernel,
        out_shape=(
            jax.ShapeDtypeStruct((RANK, COLS), f32),
            jax.ShapeDtypeStruct((FEAT, 512), bf16),
            jax.ShapeDtypeStruct((NX, 8, 128), f32),
            jax.ShapeDtypeStruct((RANK, 128), f32),
            jax.ShapeDtypeStruct((64, COLS), bf16),
        ),
        in_specs=[pl.BlockSpec(memory_space=pltpu.VMEM)] * 2
        + [pl.BlockSpec(memory_space=pl.ANY)]
        + [pl.BlockSpec(memory_space=pltpu.VMEM)] * 6,
        out_specs=[pl.BlockSpec(memory_space=pltpu.VMEM)] * 5,
        scratch_shapes=[
            pltpu.VMEM((8, 8, PW), f32),
            pltpu.VMEM((8, 8, PW), f32),
            pltpu.VMEM((NZ, 8, PW), f32),
            pltpu.VMEM((8, 8, PW), f32),
            pltpu.VMEM((NX, RANK + 8, 128), f32),
            pltpu.VMEM((NX, RANK + 8, 128), f32),
            pltpu.VMEM((RANK, COLS), f32),
            pltpu.VMEM((32, COLS), f32),
            pltpu.VMEM((2, 4, 8, HALF), f32),
            pltpu.VMEM((2, 4, 8, HALF), f32),
            pltpu.VMEM((2, 4, 8, QUART), f32),
            pltpu.VMEM((2, 4, 8, QUART), f32),
            pltpu.VMEM((NZ, 2, 8, QUART), f32),
            pltpu.VMEM((2, 4, 8, QUART), f32),
            pltpu.VMEM((2, 2, 4, 8, HALF), f32),
            pltpu.VMEM((24, COLS), f32),
            pltpu.VMEM((NX, NC, 24, CB), f32),
            pltpu.VMEM((2, 24, CB), f32),
            pltpu.VMEM((NZ, NY, NX, 48, CB), bf16),
            pltpu.VMEM((NC, NX, 256, FEAT), bf16),
            pltpu.VMEM((FEAT, CB), bf16),
            pltpu.VMEM((FEAT, CB), bf16),
            pltpu.VMEM((NC, 256, CB), f32),
            pltpu.VMEM((NC, 256, CB), f32),
            pltpu.VMEM((NX, NC, RANK, 128), f32),
            pltpu.VMEM((NC, 256, 256), bf16),
            pltpu.VMEM((256, CB), f32),
            pltpu.VMEM((NX, NC, 64, CB), bf16),
            pltpu.VMEM((NX, NC, 64, CB), bf16),
            pltpu.VMEM((FEAT, COLS), bf16),
            pltpu.VMEM((8, 128), f32),
            pltpu.VMEM((COLS // HEAD, 128), f32),
            pltpu.SemaphoreType.DMA((LOADS,)),
            pltpu.SemaphoreType.DMA((copies,)),
            pltpu.SemaphoreType.DMA((copies,)),
        ],
        compiler_params=pltpu.CompilerParams(
            collective_id=0, has_side_effects=True, vmem_limit_bytes=56 * 2**20
        ),
        name="step",
    )(x, g, e, factor, w, v, b, bv, flags)


def finish_kernel(
    flags_ref, left_ref, g_ref, e_ref, qt_ref, sums_ref, own_ref, next_ref, w_ref, v_ref, b_ref, bv_ref,
    error_ref, weight_ref, velocity_ref, bias_ref, bias_velocity_ref, factor_ref, out_ref,
):
    f32, bf16 = jnp.float32, jnp.bfloat16
    highest = lax.Precision.HIGHEST
    step = pl.program_id(0)
    groups = COLS // HEAD

    @pl.when(step == 0)
    def _():
        total = jnp.concatenate(
            [sums_ref[k, r : r + 1, :] for k in range(NX) for r in range(FEAT // 128)], axis=1
        )
        gb = total * (1.0 / (256 * 64))
        b = b_ref[...]
        nb = jnp.sqrt(jnp.sum(b * b, keepdims=True))
        ng = jnp.sqrt(jnp.sum(gb * gb, keepdims=True))
        skip = flags_ref[groups] == 1
        rb = jnp.where(skip, 1.0, trust_coef * nb / (ng + decay_coef * nb))
        db = jnp.where(skip, 0.0, decay_coef)
        bv = momentum_coef * bv_ref[...] + learn_rate * rb * (gb + db * b)
        bias_velocity_ref[...] = bv
        bias_ref[...] = b - bv

    q = qt_ref[...]
    hi = q.astype(bf16)
    lo = (q - hi.astype(f32)).astype(bf16)
    right = jnp.concatenate([g_ref[...], hi, hi, lo, jnp.zeros_like(hi)], axis=0)
    error_ref[...] = (nn(left_ref[...], right) + e_ref[...].astype(f32)).astype(bf16)
    factor_ref[...] = hi
    out_ref[...] = next_ref[...]

    both = lax.dot_general(
        own_ref[...], q, (((0,), (0,)), ((), ())), precision=highest, preferred_element_type=f32
    )
    own = w_ref.shape[0]
    norms = sums_ref[0, 6:7] + sums_ref[1, 6:7] + sums_ref[2, 6:7] + sums_ref[3, 6:7]
    lane = lax.broadcasted_iota(jnp.int32, (1, 128), 1)
    per = TILE // HEAD
    for j in range(per):
        cols = slice(j * HEAD, (j + 1) * HEAD)
        head = step * per + j
        nw = jnp.sqrt(jnp.sum(jnp.where(lane == head, norms, 0.0), keepdims=True))
        na = jnp.sqrt(jnp.sum(q[:, cols] * q[:, cols], keepdims=True))
        skip = flags_ref[head] == 1
        rate = jnp.where(skip, 1.0, trust_coef * nw / (na + decay_coef * nw))
        decay = jnp.where(skip, 0.0, decay_coef)
        w = w_ref[:, 0, cols]
        v = momentum_coef * v_ref[:, 0, cols] + learn_rate * rate * (both[0:own, cols] + decay * w)
        velocity_ref[:, 0, cols] = v
        weight_ref[:, 0, cols] = w - v


def finish_call(flags, left, g, e, qt, sums, own, out, w, v, b, bv):
    f32, bf16 = jnp.float32, jnp.bfloat16

    def whole(a):
        return pl.BlockSpec(a.shape, lambda i: (0,) * a.ndim)

    def tiled(a):
        return pl.BlockSpec(a.shape[:-1] + (TILE,), lambda i: (0,) * (a.ndim - 1) + (i,))

    return pl.pallas_call(
        finish_kernel,
        grid=(COLS // TILE,),
        out_shape=(
            jax.ShapeDtypeStruct(e.shape, bf16),
            jax.ShapeDtypeStruct(w.shape, f32),
            jax.ShapeDtypeStruct(v.shape, f32),
            jax.ShapeDtypeStruct(b.shape, f32),
            jax.ShapeDtypeStruct(bv.shape, f32),
            jax.ShapeDtypeStruct((RANK, COLS), bf16),
            jax.ShapeDtypeStruct(out.shape, bf16),
        ),
        in_specs=[
            pl.BlockSpec(memory_space=pltpu.SMEM),
            whole(left), tiled(g), tiled(e), tiled(qt), whole(sums), whole(own), tiled(out),
            tiled(w), tiled(v), whole(b), whole(bv),
        ],
        out_specs=(
            tiled(e), tiled(w), tiled(v), whole(b), whole(bv),
            tiled(qt), tiled(out),
        ),
        compiler_params=pltpu.CompilerParams(vmem_limit_bytes=60 * 2**20),
        name="finish",
    )(flags, left, g, e, qt, sums, own, out, w, v, b, bv)


def shards(inputs, out_grads, error, weight, velocity, bias, bias_velocity, start_factor, flags):
    w, v = weight.transpose(1, 0, 2), velocity.transpose(1, 0, 2)
    b, bv = bias.reshape(1, COLS), bias_velocity.reshape(1, COLS)
    qt, left, sums, own, out = step_call(
        inputs, out_grads, error[0], start_factor.T, w, v, b, bv, flags.reshape(1, flags.shape[0])
    )
    error_new, weight_new, velocity_new, bias_new, bias_velocity_new, factor_new, next_out = finish_call(
        flags, left, out_grads, error[0], qt, sums, own, out, w, v, b, bv
    )
    return (
        error_new[None],
        weight_new.transpose(1, 0, 2),
        velocity_new.transpose(1, 0, 2),
        bias_new.reshape(COLS),
        bias_velocity_new.reshape(COLS),
        factor_new.T,
        next_out,
    )


def solution(mesh):
    in_specs = (
        P("dp", "fsdp"),
        P("dp", None),
        P("dp", "fsdp", None),
        P("fsdp", "dp", None),
        P("fsdp", "dp", None),
        P(),
        P(),
        P(),
        P(),
    )
    out_specs = (
        P("dp", "fsdp", None),
        P("fsdp", "dp", None),
        P("fsdp", "dp", None),
        P(),
        P(),
        P(),
        P(("dp", "fsdp"), None),
    )
    return jax.shard_map(shards, mesh=mesh, in_specs=in_specs, out_specs=out_specs, check_vma=False)
```

```python
import jax
import jax.numpy as jnp
from jax import lax
from jax.experimental import pallas as pl
from jax.experimental.pallas import tpu as pltpu
from jax.sharding import PartitionSpec as P

HEAD = 128
MESH = pl.DeviceIdType.MESH

trust_coef = 0.02
decay_coef = 0.0001
momentum_coef = 0.9
learn_rate = 4.0

NX, NY, NZ, NC = 4, 4, 8, 2
RANK = 64
FEAT = 768
COLS = 3072
PW = FEAT + 128
HALF = COLS // 2
QUART = HALF // 4
CB = FEAT // NC
LOADS = 3
TILE = 768


def nt(a, b):
    return lax.dot_general(a, b, (((1,), (1,)), ((), ())), preferred_element_type=jnp.float32)


def nn(a, b):
    return lax.dot_general(a, b, (((1,), (0,)), ((), ())), preferred_element_type=jnp.float32)


def pieces(a):
    hi = a.astype(jnp.bfloat16)
    lo = (a - hi.astype(jnp.float32)).astype(jnp.bfloat16)
    return jnp.concatenate([hi, lo], axis=0)


def fold(a):
    n = a.shape[0] // 2
    return a[:n] + a[n:]


def eliminate(work, start, stop):
    n = work.shape[0]
    rows = lax.broadcasted_iota(jnp.int32, (n, 2 * n), 0)
    first = lax.broadcasted_iota(jnp.int32, (n, 1), 0)
    for k in range(start, stop):
        pivot = work[k : k + 1, k : k + 1]
        inv = lax.rsqrt(pivot)
        inv = inv * (1.5 - 0.5 * pivot * inv * inv)
        row = work[k : k + 1, :] * inv
        col = jnp.where(first > k, work[:, k : k + 1] * inv, 0.0)
        work = jnp.where(rows == k, row, work - col * row)
    return work


def beside_identity(gram):
    n = gram.shape[0]
    rows = lax.broadcasted_iota(jnp.int32, (n, n), 0)
    cols = lax.broadcasted_iota(jnp.int32, (n, n), 1)
    return jnp.concatenate([gram, jnp.where(rows == cols, 1.0, 0.0).astype(jnp.float32)], axis=1)


def step_kernel(
    x_ref, g_ref, e_hbm, s_ref, w_ref, v_ref, b_ref, bv_ref, flags_ref,
    qt_ref, left_ref, sums_ref, own_ref, out_ref,
    ppart, precv, pz, pfull, gsend, gx,
    zpart, zc, zsum, z1, z1s, z2, zz, z3, zfull,
    wv, wrecv, stage, wbuf, xall, wh, wt, ya, yb, xph, tokens, moved, osend, orecv,
    e_ref, extra, heads, load_sem, send_sem, recv_sem,
):
    f32, bf16 = jnp.float32, jnp.bfloat16
    dp = lax.axis_index("dp")
    x = lax.axis_index("fsdp")
    z, y, c = dp // (NY * NC), (dp // NC) % NY, dp % NC
    yc = y * NC + c

    def at_yc(k):
        return (z * NY * NC + k, x)

    def at_z(k):
        return (k * NY * NC + yc, x)

    def at_x(k):
        return (dp, k)

    def at_y(k):
        return (z * NY * NC + k * NC + c, x)

    def at_xc(k, core):
        return (z * NY * NC + y * NC + core, k)

    yc_peers = [lax.rem(yc + k, NY * NC) for k in range(1, NY * NC)]
    z_peers = [lax.rem(z + k, NZ) for k in range(1, NZ)]
    x_peers = [lax.rem(x + k, NX) for k in range(1, NX)]
    y_peers = [lax.rem(y + k, NY) for k in range(1, NY)]
    xc_peers = [(x, 1 - c)] + [(k, core) for k in x_peers for core in (c, 1 - c)]
    other = at_xc(x, 1 - c)

    barrier = pltpu.get_barrier_semaphore()
    greet = [at_yc(k) for k in yc_peers] + [at_z(k) for k in z_peers]
    greet += [at_xc(k, core) for k in x_peers for core in (c, 1 - c)]
    for d in greet:
        pl.semaphore_signal(barrier, inc=1, device_id=d, device_id_type=MESH)

    count = [0]
    sent = []

    def send(src, dst, device):
        i = count[0]
        count[0] += 1
        copy = pltpu.make_async_remote_copy(
            src_ref=src, dst_ref=dst, send_sem=send_sem.at[i], recv_sem=recv_sem.at[i],
            device_id=device, device_id_type=MESH,
        )
        copy.start()
        sent.append(copy)
        return copy

    def arrive(copies):
        for copy in copies:
            copy.wait_recv()

    own = w_ref.shape[0]
    rows = FEAT // LOADS
    loads = []
    for k in range(LOADS):
        block = pl.ds(k * rows, rows)
        loads.append(pltpu.make_async_copy(e_hbm.at[block], e_ref.at[block], load_sem.at[k]))
        loads[k].start()
    w = w_ref[:, 0, :]
    wv[0:own] = w
    wv[own : 2 * own] = v_ref[:, 0, :]
    xall[c, x] = x_ref[...]

    ones = jnp.ones((8, x_ref.shape[0]), bf16)
    column_sums = nn(ones, g_ref[:, pl.ds(pl.multiple_of(x * FEAT, 128), FEAT)])
    squares = jnp.sum(w * w, axis=0, keepdims=True)
    groups = COLS // HEAD
    for k in range(groups):
        heads[k : k + 1] = squares[:, k * HEAD : (k + 1) * HEAD]
    lane = lax.broadcasted_iota(jnp.int32, (groups, 128), 1)
    row = lax.broadcasted_iota(jnp.int32, (groups, 128), 0)
    norms = jnp.where(lane == row, jnp.sum(heads[...], axis=1, keepdims=True), 0.0)
    extra[...] = jnp.zeros_like(extra)
    for k in range(FEAT // 128):
        extra[k : k + 1] = column_sums[0:1, k * 128 : (k + 1) * 128]
    extra[6:7] = jnp.sum(norms, axis=0, keepdims=True)

    factor = s_ref[...].T
    gst = nn(g_ref[...], factor).T
    pt = fold(nn(pieces(gst), x_ref[...])) * (1.0 / x_ref.shape[0])
    pl.semaphore_wait(barrier, len(greet))

    def cols_of(k, core):
        return wv.at[:, pl.ds(pl.multiple_of(k * FEAT + core * CB, 128), CB)]

    wv_copies = [send(cols_of(k, core), wrecv.at[x, c], at_xc(k, core)) for k, core in xc_peers]
    wrecv[x, c] = wv[:, pl.ds(pl.multiple_of(x * FEAT + c * CB, 128), CB)]

    for k in range(LOADS):
        loads[k].wait()
        cols = slice(k * rows, (k + 1) * rows)
        part = pt[:, cols] + nn(e_ref[cols], factor).T
        for i in range(NY * NC):
            ppart[i, :, cols] = part[8 * i : 8 * i + 8]
    for i in range(NY * NC):
        ppart[i, :, FEAT:PW] = extra[...]
    copies = [send(ppart.at[k], precv.at[yc], at_yc(k)) for k in yc_peers]
    precv[yc] = ppart[yc]

    def first_half(iz, part, n):
        return wbuf.at[iz, :, pl.ds(part, n)]

    def small(iz, part, n):
        return wbuf.at[iz, y, pl.ds(2 + part, n)]

    def ring(chunk, step):
        last = step == NZ // 2 - 1
        up = chunk(lax.rem(z - step + NZ, NZ), 0, 1 if last else 2)
        down = chunk(lax.rem(z + step, NZ), 1 if last else 0, 1 if last else 2)
        return [send(up, up, at_z(lax.rem(z + 1, NZ))), send(down, down, at_z(lax.rem(z + NZ - 1, NZ)))]

    def pack():
        arrive(wv_copies)
        for k in range(NX):
            first, second = wrecv[k, 0], wrecv[k, 1]
            stage[0, 0:own] = first[0:own]
            stage[0, own : 2 * own] = second[0:own]
            stage[1, 0:own] = first[own : 2 * own]
            stage[1, own : 2 * own] = second[own : 2 * own]
            full = stage[0]
            high = full.astype(bf16).astype(f32)
            rest = full - high - momentum_coef * stage[1]
            wbuf[z, y, k] = jnp.concatenate([high, rest], axis=0).astype(bf16)
        piece = wbuf.at[z, y, pl.ds(0, 2)]
        return [send(piece, piece, at_y(k)) for k in y_peers], ring(small, 0)

    def column(iy, ix, n):
        return wbuf.at[:, iy, pl.ds(ix, n)]

    def deinterleave(k):
        for iz in range(NZ):
            for iy in range(0, NY, 2):
                u0 = wbuf[iz, iy, k].astype(f32)
                u1 = wbuf[iz, iy + 1, k].astype(f32)
                row = iz * 96 + iy * 24
                wh[row : row + 48] = jnp.concatenate([u0[0:24], u1[0:24]], axis=0).astype(bf16)
                wt[row : row + 48] = jnp.concatenate([u0[24:48], u1[24:48]], axis=0).astype(bf16)

    def products(k, first):
        deinterleave(k)
        for core in range(NC):
            a = nn(xall[core, k], wh[...])
            b = nn(xall[core, k], wt[...])
            ya[core] = a if first else ya[core] + a
            yb[core] = b if first else yb[core] + b

    a_copies, b_copies = pack()

    arrive(copies)
    total = precv[0]
    for k in range(1, NY * NC):
        total = total + precv[k]
    pz[z] = total
    copies = [send(pz.at[z], pz.at[z], at_z(k)) for k in z_peers]
    arrive(b_copies)
    b_copies = ring(small, 1)
    arrive(a_copies)
    a_copies = ring(first_half, 0)
    x_copies = [send(x_ref, xall.at[c, x], at_x(k)) for k in x_peers]
    arrive(copies[:2] + copies[-2:])
    arrive(b_copies)
    b_copies = ring(small, 2)
    arrive(copies[2:-2])
    total = pz[0]
    for k in range(1, NZ):
        total = total + pz[k]
    pfull[yc] = total
    copies = [send(pfull.at[yc], pfull.at[yc], at_yc(k)) for k in yc_peers]
    arrive(b_copies)
    b_copies = ring(small, 3)
    arrive(copies[:1] + copies[-1:])
    arrive(b_copies)
    b_copies = [send(column(y, 2, 2), column(y, 2, 2), at_y(lax.rem(y + k, NY))) for k in (1, NY - 1)]
    arrive(copies[1:-1])

    ptot = pfull[...].reshape(RANK, PW)
    pt = ptot[:, 0:FEAT]
    pp = pieces(pt)
    xpt = fold(nt(pp, x_ref[...]))
    gram = lax.dot_general(
        pt, pt, (((1,), (1,)), ((), ())), precision=lax.Precision.HIGHEST,
        preferred_element_type=f32,
    )
    for k in range(NX):
        gsend[k, 0:RANK, 0:RANK] = gram
        gsend[k, 0:RANK, RANK:] = xpt[:, k * 64 : (k + 1) * 64]
        gsend[k, RANK:, :] = ptot[0:8, FEAT:]
    gram_copies = [send(gsend.at[k], gx.at[x], at_x(k)) for k in x_peers]
    gx[x] = gsend[x]
    arrive(a_copies)
    a_copies = ring(first_half, 1)

    zpart[...] = fold(nn(pieces(xpt), g_ref[...])) * (1.0 / x_ref.shape[0]) + fold(nn(pp, e_ref[...]))

    core_copy = send(zpart.at[pl.ds(pl.multiple_of((1 - c) * 32, 8), 32)], zc, other)
    arrive([core_copy])
    mine = zpart[pl.ds(pl.multiple_of(c * 32, 8), 32)] + zc[...]
    for k in range(4):
        zsum[0, k] = mine[8 * k : 8 * k + 8, :HALF]
        zsum[1, k] = mine[8 * k : 8 * k + 8, HALF:]
    axes = (((x, x_peers, at_x), (y, y_peers, at_y)),) * 2
    copies = []
    for h in range(2):
        me, peers, at = axes[h][0]
        copies += [send(zsum.at[h, k], z1.at[h, me], at(k)) for k in peers]
        z1[h, me] = zsum[h, me]
    arrive(a_copies)
    a_copies = ring(first_half, 2)

    arrive(gram_copies)
    both = gx[0, 0:RANK] + gx[1, 0:RANK] + gx[2, 0:RANK] + gx[3, 0:RANK]
    for k in range(NX):
        sums_ref[k] = gx[k, RANK:, :]
    work = eliminate(beside_identity(both[:, 0:RANK]), 0, 24)
    arrive(copies)
    copies = []
    for h in range(2):
        me, peers, at = axes[h][1]
        total = z1[h, 0] + z1[h, 1] + z1[h, 2] + z1[h, 3]
        for k in range(4):
            z1s[h, k] = total[:, k * QUART : (k + 1) * QUART]
        copies += [send(z1s.at[h, k], z2.at[h, me], at(k)) for k in peers]
        z2[h, me] = z1s[h, me]
    work = eliminate(work, 24, 40)
    arrive(copies)
    for h in range(2):
        zz[z, h] = z2[h, 0] + z2[h, 1] + z2[h, 2] + z2[h, 3]
    copies = [send(zz.at[z], zz.at[z], at_z(k)) for k in z_peers]
    arrive(x_copies)
    x_core = send(xall.at[c], xall.at[c], other)
    arrive(a_copies)
    a_copies = ring(first_half, 3)
    arrive(b_copies)
    b_copies = [
        send(column(lax.rem(y + 1, NY), 2, 1), column(lax.rem(y + 1, NY), 2, 1), at_y(lax.rem(y + NY - 1, NY))),
        send(column(lax.rem(y + NY - 1, NY), 3, 1), column(lax.rem(y + NY - 1, NY), 3, 1), at_y(lax.rem(y + 1, NY))),
    ]
    inverse = eliminate(work, 40, RANK)[:, RANK:]
    ih = inverse.astype(bf16)
    il = (inverse - ih.astype(f32)).astype(bf16)
    inverse3 = jnp.concatenate([ih, ih, il], axis=1)

    def times_inverse(a):
        hi = a.astype(bf16)
        lo = (a - hi.astype(f32)).astype(bf16)
        return nn(inverse3, jnp.concatenate([hi, lo, hi], axis=0))

    xph[x, c] = times_inverse(both)
    token_copies = [send(xph.at[x, c], xph.at[x, c], at_xc(k, core)) for k, core in xc_peers]
    arrive(copies)
    total = zz[0]
    for k in range(1, NZ):
        total = total + zz[k]
    copies = []
    for h in range(2):
        me, peers, at = axes[h][1]
        z3[h, me] = total[h]
        copies += [send(z3.at[h, me], z3.at[h, me], at(k)) for k in peers]

    b, bv = b_ref[...], bv_ref[...]
    nb = jnp.sqrt(jnp.sum(b * b, keepdims=True))
    ng = jnp.zeros((1, 1), f32)
    for k in range(NX):
        gb = sums_ref[k, 0:6, :] * (1.0 / (256 * 64))
        ng = ng + jnp.sum(gb * gb, keepdims=True)
    ng = jnp.sqrt(ng)
    lane = lax.broadcasted_iota(jnp.int32, (1, flags_ref.shape[1]), 1)

    def skips(index):
        return jnp.sum(jnp.where(lane == index, flags_ref[...], 0), keepdims=True) == 1

    rb = jnp.where(skips(groups), 1.0, trust_coef * nb / (ng + decay_coef * nb))
    db = jnp.where(skips(groups), 0.0, decay_coef)
    biases = []
    for j in range(CB // HEAD):
        cols = pl.ds(pl.multiple_of(x * FEAT + c * CB + j * HEAD, HEAD), HEAD)
        gb = sums_ref[x, pl.ds(c * (CB // HEAD) + j, 1), :] * (1.0 / (256 * 64))
        biases.append(b_ref[:, cols] - momentum_coef * bv_ref[:, cols] - learn_rate * rb * (gb + db * b_ref[:, cols]))

    arrive(b_copies + [x_core])
    products(2, True)
    arrive(copies)
    copies = []
    for h in range(2):
        me, peers, at = axes[h][0]
        for k in range(4):
            zfull[c, h, me, :, k * QUART : (k + 1) * QUART] = z3[h, k]
        copies += [send(zfull.at[c, h, me], zfull.at[c, h, me], at(k)) for k in peers]
    products(3, False)
    arrive(a_copies)
    products(0, False)
    arrive(copies)
    copies = [send(zfull.at[c], zfull.at[c], other)]
    products(1, False)
    arrive(token_copies)
    for core in range(NC):
        for k in range(NX):
            part = xph[k, core].T[64:128]
            high = part.astype(bf16).astype(f32)
            tokens[core, k * 64 : (k + 1) * 64] = jnp.concatenate(
                [high, part - high, high, jnp.zeros_like(part)], axis=1
            ).astype(bf16)
    arrive(copies)

    cols = pl.ds(pl.multiple_of(lax.rem(x, 2) * FEAT + c * CB, 128), CB)
    zt = jnp.concatenate([zfull[core, x // 2, :, :, cols].reshape(32, CB) for core in range(NC)], axis=0)
    qc = times_inverse(zt) * (1.0 / (NC * NY * NZ))
    qh = qc.astype(bf16)
    ql = (qc - qh.astype(f32)).astype(bf16)
    right = jnp.concatenate([qh, qh, ql, jnp.zeros_like(qh)], axis=0)
    norms = sums_ref[0, 6:7] + sums_ref[1, 6:7] + sums_ref[2, 6:7] + sums_ref[3, 6:7]
    lanes = lax.broadcasted_iota(jnp.int32, (1, 128), 1)
    rates, decays = [], []
    for j in range(CB // HEAD):
        head = x * (FEAT // HEAD) + c * (CB // HEAD) + j
        part = qc[:, j * HEAD : (j + 1) * HEAD]
        nw = jnp.sqrt(jnp.sum(jnp.where(lanes == head, norms, 0.0), keepdims=True))
        na = jnp.sqrt(jnp.sum(part * part, keepdims=True))
        skip = skips(head)
        rates.append(learn_rate * jnp.where(skip, 1.0, trust_coef * nw / (na + decay_coef * nw)))
        decays.append(jnp.where(skip, 0.0, decay_coef))
    out_copies = []
    for core in (1 - c, c):
        moved[...] = nn(tokens[core], right)
        for j in range(CB // HEAD):
            cols = slice(j * HEAD, (j + 1) * HEAD)
            a = ya[core, :, cols]
            value = a + yb[core, :, cols] - rates[j] * (moved[:, cols] + decays[j] * a) + biases[j]
            for k in range(NX):
                osend[k, core, :, cols] = value[k * 64 : (k + 1) * 64].astype(bf16)
        for k in x_peers:
            out_copies.append(send(osend.at[k, core], orecv.at[x, c], at_xc(k, core)))
    out_copies.append(send(osend.at[x, 1 - c], orecv.at[x, c], other))
    orecv[x, c] = osend[x, c]

    for h in range(2):
        zt = jnp.concatenate([zfull[0, h].reshape(32, HALF), zfull[1, h].reshape(32, HALF)], axis=0)
        qt_ref[:, h * HALF : (h + 1) * HALF] = times_inverse(zt) * (1.0 / (NC * NY * NZ))
    left_ref[:, 0:256] = (x_ref[...].astype(f32) * (1.0 / 256)).T.astype(bf16)
    hat = times_inverse(pt)
    high = hat.astype(bf16).astype(f32)
    left_ref[:, 256:512] = jnp.concatenate([-high, high - hat, -high, jnp.zeros_like(hat)], axis=0).T.astype(bf16)
    feature = lax.broadcasted_iota(jnp.int32, (FEAT, 128), 0)
    wanted = lax.broadcasted_iota(jnp.int32, (FEAT, 128), 1)
    pick = jnp.where((feature == dp * own + wanted) & (wanted < own), 1.0, 0.0).astype(f32)
    own_ref[...] = jnp.dot(hat, pick, precision=lax.Precision.HIGHEST, preferred_element_type=f32)
    arrive(out_copies)
    for k in range(NX):
        for core in range(NC):
            out_ref[:, k * FEAT + core * CB : k * FEAT + core * CB + CB] = orecv[k, core]
    for copy in sent:
        copy.wait_send()


def step_call(x, g, e, factor, w, v, b, bv, flags):
    f32, bf16 = jnp.float32, jnp.bfloat16
    copies = 128
    return pl.pallas_call(
        step_kernel,
        out_shape=(
            jax.ShapeDtypeStruct((RANK, COLS), f32),
            jax.ShapeDtypeStruct((FEAT, 512), bf16),
            jax.ShapeDtypeStruct((NX, 8, 128), f32),
            jax.ShapeDtypeStruct((RANK, 128), f32),
            jax.ShapeDtypeStruct((64, COLS), bf16),
        ),
        in_specs=[pl.BlockSpec(memory_space=pltpu.VMEM)] * 2
        + [pl.BlockSpec(memory_space=pl.ANY)]
        + [pl.BlockSpec(memory_space=pltpu.VMEM)] * 6,
        out_specs=[pl.BlockSpec(memory_space=pltpu.VMEM)] * 5,
        scratch_shapes=[
            pltpu.VMEM((8, 8, PW), f32),
            pltpu.VMEM((8, 8, PW), f32),
            pltpu.VMEM((NZ, 8, PW), f32),
            pltpu.VMEM((8, 8, PW), f32),
            pltpu.VMEM((NX, RANK + 8, 128), f32),
            pltpu.VMEM((NX, RANK + 8, 128), f32),
            pltpu.VMEM((RANK, COLS), f32),
            pltpu.VMEM((32, COLS), f32),
            pltpu.VMEM((2, 4, 8, HALF), f32),
            pltpu.VMEM((2, 4, 8, HALF), f32),
            pltpu.VMEM((2, 4, 8, QUART), f32),
            pltpu.VMEM((2, 4, 8, QUART), f32),
            pltpu.VMEM((NZ, 2, 8, QUART), f32),
            pltpu.VMEM((2, 4, 8, QUART), f32),
            pltpu.VMEM((2, 2, 4, 8, HALF), f32),
            pltpu.VMEM((24, COLS), f32),
            pltpu.VMEM((NX, NC, 24, CB), f32),
            pltpu.VMEM((2, 24, CB), f32),
            pltpu.VMEM((NZ, NY, NX, 48, CB), bf16),
            pltpu.VMEM((NC, NX, 256, FEAT), bf16),
            pltpu.VMEM((FEAT, CB), bf16),
            pltpu.VMEM((FEAT, CB), bf16),
            pltpu.VMEM((NC, 256, CB), f32),
            pltpu.VMEM((NC, 256, CB), f32),
            pltpu.VMEM((NX, NC, RANK, 128), f32),
            pltpu.VMEM((NC, 256, 256), bf16),
            pltpu.VMEM((256, CB), f32),
            pltpu.VMEM((NX, NC, 64, CB), bf16),
            pltpu.VMEM((NX, NC, 64, CB), bf16),
            pltpu.VMEM((FEAT, COLS), bf16),
            pltpu.VMEM((8, 128), f32),
            pltpu.VMEM((COLS // HEAD, 128), f32),
            pltpu.SemaphoreType.DMA((LOADS,)),
            pltpu.SemaphoreType.DMA((copies,)),
            pltpu.SemaphoreType.DMA((copies,)),
        ],
        compiler_params=pltpu.CompilerParams(
            collective_id=0, has_side_effects=True, vmem_limit_bytes=56 * 2**20
        ),
        name="step",
    )(x, g, e, factor, w, v, b, bv, flags)


def finish_kernel(
    flags_ref, left_ref, g_ref, e_ref, qt_ref, sums_ref, own_ref, next_ref, w_ref, v_ref, b_ref, bv_ref,
    error_ref, weight_ref, velocity_ref, bias_ref, bias_velocity_ref, factor_ref, out_ref,
):
    f32, bf16 = jnp.float32, jnp.bfloat16
    highest = lax.Precision.HIGHEST
    step = pl.program_id(0)
    groups = COLS // HEAD

    @pl.when(step == 0)
    def _():
        total = jnp.concatenate(
            [sums_ref[k, r : r + 1, :] for k in range(NX) for r in range(FEAT // 128)], axis=1
        )
        gb = total * (1.0 / (256 * 64))
        b = b_ref[...]
        nb = jnp.sqrt(jnp.sum(b * b, keepdims=True))
        ng = jnp.sqrt(jnp.sum(gb * gb, keepdims=True))
        skip = flags_ref[groups] == 1
        rb = jnp.where(skip, 1.0, trust_coef * nb / (ng + decay_coef * nb))
        db = jnp.where(skip, 0.0, decay_coef)
        bv = momentum_coef * bv_ref[...] + learn_rate * rb * (gb + db * b)
        bias_velocity_ref[...] = bv
        bias_ref[...] = b - bv

    q = qt_ref[...]
    hi = q.astype(bf16)
    lo = (q - hi.astype(f32)).astype(bf16)
    right = jnp.concatenate([g_ref[...], hi, hi, lo, jnp.zeros_like(hi)], axis=0)
    error_ref[...] = (nn(left_ref[...], right) + e_ref[...].astype(f32)).astype(bf16)
    factor_ref[...] = hi
    out_ref[...] = next_ref[...]

    both = lax.dot_general(
        own_ref[...], q, (((0,), (0,)), ((), ())), precision=highest, preferred_element_type=f32
    )
    own = w_ref.shape[0]
    norms = sums_ref[0, 6:7] + sums_ref[1, 6:7] + sums_ref[2, 6:7] + sums_ref[3, 6:7]
    lane = lax.broadcasted_iota(jnp.int32, (1, 128), 1)
    per = TILE // HEAD
    for j in range(per):
        cols = slice(j * HEAD, (j + 1) * HEAD)
        head = step * per + j
        nw = jnp.sqrt(jnp.sum(jnp.where(lane == head, norms, 0.0), keepdims=True))
        na = jnp.sqrt(jnp.sum(q[:, cols] * q[:, cols], keepdims=True))
        skip = flags_ref[head] == 1
        rate = jnp.where(skip, 1.0, trust_coef * nw / (na + decay_coef * nw))
        decay = jnp.where(skip, 0.0, decay_coef)
        w = w_ref[:, 0, cols]
        v = momentum_coef * v_ref[:, 0, cols] + learn_rate * rate * (both[0:own, cols] + decay * w)
        velocity_ref[:, 0, cols] = v
        weight_ref[:, 0, cols] = w - v


def finish_call(flags, left, g, e, qt, sums, own, out, w, v, b, bv):
    f32, bf16 = jnp.float32, jnp.bfloat16

    def whole(a):
        return pl.BlockSpec(a.shape, lambda i: (0,) * a.ndim)

    def tiled(a):
        return pl.BlockSpec(a.shape[:-1] + (TILE,), lambda i: (0,) * (a.ndim - 1) + (i,))

    return pl.pallas_call(
        finish_kernel,
        grid=(COLS // TILE,),
        out_shape=(
            jax.ShapeDtypeStruct(e.shape, bf16),
            jax.ShapeDtypeStruct(w.shape, f32),
            jax.ShapeDtypeStruct(v.shape, f32),
            jax.ShapeDtypeStruct(b.shape, f32),
            jax.ShapeDtypeStruct(bv.shape, f32),
            jax.ShapeDtypeStruct((RANK, COLS), bf16),
            jax.ShapeDtypeStruct(out.shape, bf16),
        ),
        in_specs=[
            pl.BlockSpec(memory_space=pltpu.SMEM),
            whole(left), tiled(g), tiled(e), tiled(qt), whole(sums), whole(own), tiled(out),
            tiled(w), tiled(v), whole(b), whole(bv),
        ],
        out_specs=(
            tiled(e), tiled(w), tiled(v), whole(b), whole(bv),
            tiled(qt), tiled(out),
        ),
        compiler_params=pltpu.CompilerParams(vmem_limit_bytes=60 * 2**20),
        name="finish",
    )(flags, left, g, e, qt, sums, own, out, w, v, b, bv)


def shards(inputs, out_grads, error, weight, velocity, bias, bias_velocity, start_factor, flags):
    w, v = weight.transpose(1, 0, 2), velocity.transpose(1, 0, 2)
    b, bv = bias.reshape(1, COLS), bias_velocity.reshape(1, COLS)
    qt, left, sums, own, out = step_call(
        inputs, out_grads, error[0], start_factor.T, w, v, b, bv, flags.reshape(1, flags.shape[0])
    )
    error_new, weight_new, velocity_new, bias_new, bias_velocity_new, factor_new, next_out = finish_call(
        flags, left, out_grads, error[0], qt, sums, own, out, w, v, b, bv
    )
    return (
        error_new[None],
        weight_new.transpose(1, 0, 2),
        velocity_new.transpose(1, 0, 2),
        bias_new.reshape(COLS),
        bias_velocity_new.reshape(COLS),
        factor_new.T,
        next_out,
    )


def solution(mesh):
    in_specs = (
        P("dp", "fsdp"),
        P("dp", None),
        P("dp", "fsdp", None),
        P("fsdp", "dp", None),
        P("fsdp", "dp", None),
        P(),
        P(),
        P(),
        P(),
    )
    out_specs = (
        P("dp", "fsdp", None),
        P("fsdp", "dp", None),
        P("fsdp", "dp", None),
        P(),
        P(),
        P(),
        P(("dp", "fsdp"), None),
    )
    return jax.shard_map(shards, mesh=mesh, in_specs=in_specs, out_specs=out_specs, check_vma=False)
```

```python
import jax
import jax.numpy as jnp
from jax import lax
from jax.experimental import pallas as pl
from jax.experimental.pallas import tpu as pltpu
from jax.sharding import PartitionSpec as P

HEAD = 128
MESH = pl.DeviceIdType.MESH

trust_coef = 0.02
decay_coef = 0.0001
momentum_coef = 0.9
learn_rate = 4.0

NX, NY, NZ, NC = 4, 4, 8, 2
RANK = 64
FEAT = 768
COLS = 3072
PW = FEAT + 128
HALF = COLS // 2
QUART = HALF // 4
CB = FEAT // NC
LOADS = 3
TILE = 768


def nt(a, b):
    return lax.dot_general(a, b, (((1,), (1,)), ((), ())), preferred_element_type=jnp.float32)


def nn(a, b):
    return lax.dot_general(a, b, (((1,), (0,)), ((), ())), preferred_element_type=jnp.float32)


def pieces(a):
    hi = a.astype(jnp.bfloat16)
    lo = (a - hi.astype(jnp.float32)).astype(jnp.bfloat16)
    return jnp.concatenate([hi, lo], axis=0)


def fold(a):
    n = a.shape[0] // 2
    return a[:n] + a[n:]


def eliminate(work, start, stop):
    n = work.shape[0]
    rows = lax.broadcasted_iota(jnp.int32, (n, 2 * n), 0)
    first = lax.broadcasted_iota(jnp.int32, (n, 1), 0)
    for k in range(start, stop):
        pivot = work[k : k + 1, k : k + 1]
        inv = lax.rsqrt(pivot)
        inv = inv * (1.5 - 0.5 * pivot * inv * inv)
        row = work[k : k + 1, :] * inv
        col = jnp.where(first > k, work[:, k : k + 1] * inv, 0.0)
        work = jnp.where(rows == k, row, work - col * row)
    return work


def beside_identity(gram):
    n = gram.shape[0]
    rows = lax.broadcasted_iota(jnp.int32, (n, n), 0)
    cols = lax.broadcasted_iota(jnp.int32, (n, n), 1)
    return jnp.concatenate([gram, jnp.where(rows == cols, 1.0, 0.0).astype(jnp.float32)], axis=1)


def step_kernel(
    x_ref, g_ref, e_hbm, s_ref, w_ref, v_ref, b_ref, bv_ref, flags_ref,
    qt_ref, left_ref, sums_ref, own_ref, out_ref,
    ppart, precv, pz, pfull, gsend, gx,
    zpart, zc, zsum, z1, z1s, z2, zz, z3, zfull,
    wv, wrecv, stage, wbuf, xall, wh, wt, ya, yb, xph, tokens, moved, osend, orecv,
    e_ref, extra, heads, load_sem, send_sem, recv_sem,
):
    f32, bf16 = jnp.float32, jnp.bfloat16
    dp = lax.axis_index("dp")
    x = lax.axis_index("fsdp")
    z, y, c = dp // (NY * NC), (dp // NC) % NY, dp % NC
    yc = y * NC + c

    def at_yc(k):
        return (z * NY * NC + k, x)

    def at_z(k):
        return (k * NY * NC + yc, x)

    def at_x(k):
        return (dp, k)

    def at_y(k):
        return (z * NY * NC + k * NC + c, x)

    def at_xc(k, core):
        return (z * NY * NC + y * NC + core, k)

    yc_peers = [lax.rem(yc + k, NY * NC) for k in range(1, NY * NC)]
    z_peers = [lax.rem(z + k, NZ) for k in range(1, NZ)]
    x_peers = [lax.rem(x + k, NX) for k in range(1, NX)]
    y_peers = [lax.rem(y + k, NY) for k in range(1, NY)]
    xc_peers = [(x, 1 - c)] + [(k, core) for k in x_peers for core in (c, 1 - c)]
    other = at_xc(x, 1 - c)

    barrier = pltpu.get_barrier_semaphore()
    greet = [at_yc(k) for k in yc_peers] + [at_z(k) for k in z_peers]
    greet += [at_xc(k, core) for k in x_peers for core in (c, 1 - c)]
    for d in greet:
        pl.semaphore_signal(barrier, inc=1, device_id=d, device_id_type=MESH)

    count = [0]
    sent = []

    def send(src, dst, device):
        i = count[0]
        count[0] += 1
        copy = pltpu.make_async_remote_copy(
            src_ref=src, dst_ref=dst, send_sem=send_sem.at[i], recv_sem=recv_sem.at[i],
            device_id=device, device_id_type=MESH,
        )
        copy.start()
        sent.append(copy)
        return copy

    def arrive(copies):
        for copy in copies:
            copy.wait_recv()

    own = w_ref.shape[0]
    rows = FEAT // LOADS
    loads = []
    for k in range(LOADS):
        block = pl.ds(k * rows, rows)
        loads.append(pltpu.make_async_copy(e_hbm.at[block], e_ref.at[block], load_sem.at[k]))
        loads[k].start()
    w = w_ref[:, 0, :]
    wv[0:own] = w
    wv[own : 2 * own] = v_ref[:, 0, :]
    xall[c, x] = x_ref[...]

    ones = jnp.ones((8, x_ref.shape[0]), bf16)
    column_sums = nn(ones, g_ref[:, pl.ds(pl.multiple_of(x * FEAT, 128), FEAT)])
    squares = jnp.sum(w * w, axis=0, keepdims=True)
    groups = COLS // HEAD
    for k in range(groups):
        heads[k : k + 1] = squares[:, k * HEAD : (k + 1) * HEAD]
    lane = lax.broadcasted_iota(jnp.int32, (groups, 128), 1)
    row = lax.broadcasted_iota(jnp.int32, (groups, 128), 0)
    norms = jnp.where(lane == row, jnp.sum(heads[...], axis=1, keepdims=True), 0.0)
    extra[...] = jnp.zeros_like(extra)
    for k in range(FEAT // 128):
        extra[k : k + 1] = column_sums[0:1, k * 128 : (k + 1) * 128]
    extra[6:7] = jnp.sum(norms, axis=0, keepdims=True)

    factor = s_ref[...].T
    gst = nn(g_ref[...], factor).T
    pt = fold(nn(pieces(gst), x_ref[...])) * (1.0 / x_ref.shape[0])
    pl.semaphore_wait(barrier, len(greet))

    def cols_of(k, core):
        return wv.at[:, pl.ds(pl.multiple_of(k * FEAT + core * CB, 128), CB)]

    wv_copies = [send(cols_of(k, core), wrecv.at[x, c], at_xc(k, core)) for k, core in xc_peers]
    wrecv[x, c] = wv[:, pl.ds(pl.multiple_of(x * FEAT + c * CB, 128), CB)]

    for k in range(LOADS):
        loads[k].wait()
        cols = slice(k * rows, (k + 1) * rows)
        part = pt[:, cols] + nn(e_ref[cols], factor).T
        for i in range(NY * NC):
            ppart[i, :, cols] = part[8 * i : 8 * i + 8]
    for i in range(NY * NC):
        ppart[i, :, FEAT:PW] = extra[...]
    copies = [send(ppart.at[k], precv.at[yc], at_yc(k)) for k in yc_peers]
    precv[yc] = ppart[yc]

    def first_half(iz, part, n):
        return wbuf.at[iz, :, pl.ds(part, n)]

    def small(iz, part, n):
        return wbuf.at[iz, y, pl.ds(2 + part, n)]

    def ring(chunk, step):
        last = step == NZ // 2 - 1
        up = chunk(lax.rem(z - step + NZ, NZ), 0, 1 if last else 2)
        down = chunk(lax.rem(z + step, NZ), 1 if last else 0, 1 if last else 2)
        return [send(up, up, at_z(lax.rem(z + 1, NZ))), send(down, down, at_z(lax.rem(z + NZ - 1, NZ)))]

    def pack():
        arrive(wv_copies)
        for k in range(NX):
            first, second = wrecv[k, 0], wrecv[k, 1]
            stage[0, 0:own] = first[0:own]
            stage[0, own : 2 * own] = second[0:own]
            stage[1, 0:own] = first[own : 2 * own]
            stage[1, own : 2 * own] = second[own : 2 * own]
            full = stage[0]
            high = full.astype(bf16).astype(f32)
            rest = full - high - momentum_coef * stage[1]
            wbuf[z, y, k] = jnp.concatenate([high, rest], axis=0).astype(bf16)
        piece = wbuf.at[z, y, pl.ds(0, 2)]
        return [send(piece, piece, at_y(k)) for k in y_peers], ring(small, 0)

    def column(iy, ix, n):
        return wbuf.at[:, iy, pl.ds(ix, n)]

    def deinterleave(k):
        for iz in range(NZ):
            for iy in range(0, NY, 2):
                u0 = wbuf[iz, iy, k].astype(f32)
                u1 = wbuf[iz, iy + 1, k].astype(f32)
                row = iz * 96 + iy * 24
                wh[row : row + 48] = jnp.concatenate([u0[0:24], u1[0:24]], axis=0).astype(bf16)
                wt[row : row + 48] = jnp.concatenate([u0[24:48], u1[24:48]], axis=0).astype(bf16)

    def products(k, first):
        deinterleave(k)
        for core in range(NC):
            a = nn(xall[core, k], wh[...])
            b = nn(xall[core, k], wt[...])
            ya[core] = a if first else ya[core] + a
            yb[core] = b if first else yb[core] + b

    a_copies, b_copies = pack()

    arrive(copies)
    total = precv[0]
    for k in range(1, NY * NC):
        total = total + precv[k]
    pz[z] = total
    copies = [send(pz.at[z], pz.at[z], at_z(k)) for k in z_peers]
    arrive(b_copies)
    b_copies = ring(small, 1)
    arrive(a_copies)
    a_copies = ring(first_half, 0)
    x_copies = [send(x_ref, xall.at[c, x], at_x(k)) for k in x_peers]
    arrive(copies[:2] + copies[-2:])
    arrive(b_copies)
    b_copies = ring(small, 2)
    arrive(copies[2:-2])
    total = pz[0]
    for k in range(1, NZ):
        total = total + pz[k]
    pfull[yc] = total
    copies = [send(pfull.at[yc], pfull.at[yc], at_yc(k)) for k in yc_peers]
    arrive(b_copies)
    b_copies = ring(small, 3)
    arrive(copies[:1] + copies[-1:])
    arrive(b_copies)
    b_copies = [send(column(y, 2, 2), column(y, 2, 2), at_y(lax.rem(y + k, NY))) for k in (1, NY - 1)]
    arrive(copies[1:-1])

    ptot = pfull[...].reshape(RANK, PW)
    pt = ptot[:, 0:FEAT]
    pp = pieces(pt)
    xpt = fold(nt(pp, x_ref[...]))
    gram = lax.dot_general(
        pt, pt, (((1,), (1,)), ((), ())), precision=lax.Precision.HIGHEST,
        preferred_element_type=f32,
    )
    for k in range(NX):
        gsend[k, 0:RANK, 0:RANK] = gram
        gsend[k, 0:RANK, RANK:] = xpt[:, k * 64 : (k + 1) * 64]
        gsend[k, RANK:, :] = ptot[0:8, FEAT:]
    gram_copies = [send(gsend.at[k], gx.at[x], at_x(k)) for k in x_peers]
    gx[x] = gsend[x]
    arrive(a_copies)
    a_copies = ring(first_half, 1)

    zpart[...] = fold(nn(pieces(xpt), g_ref[...])) * (1.0 / x_ref.shape[0]) + fold(nn(pp, e_ref[...]))

    core_copy = send(zpart.at[pl.ds(pl.multiple_of((1 - c) * 32, 8), 32)], zc, other)
    arrive([core_copy])
    mine = zpart[pl.ds(pl.multiple_of(c * 32, 8), 32)] + zc[...]
    for k in range(4):
        zsum[0, k] = mine[8 * k : 8 * k + 8, :HALF]
        zsum[1, k] = mine[8 * k : 8 * k + 8, HALF:]
    copies = [send(zsum.at[:, k], z1.at[:, x], at_x(k)) for k in x_peers]
    z1[:, x] = zsum[:, x]
    arrive(a_copies)
    a_copies = ring(first_half, 2)

    arrive(gram_copies)
    both = gx[0, 0:RANK] + gx[1, 0:RANK] + gx[2, 0:RANK] + gx[3, 0:RANK]
    for k in range(NX):
        sums_ref[k] = gx[k, RANK:, :]
    work = eliminate(beside_identity(both[:, 0:RANK]), 0, 24)
    arrive(copies)
    for h in range(2):
        total = z1[h, 0] + z1[h, 1] + z1[h, 2] + z1[h, 3]
        for k in range(4):
            z1s[h, k] = total[:, k * QUART : (k + 1) * QUART]
    copies = [send(z1s.at[:, k], z2.at[:, y], at_y(k)) for k in y_peers]
    z2[:, y] = z1s[:, y]
    work = eliminate(work, 24, 40)
    arrive(copies)
    for h in range(2):
        zz[z, h] = z2[h, 0] + z2[h, 1] + z2[h, 2] + z2[h, 3]
    copies = [send(zz.at[z], zz.at[z], at_z(k)) for k in z_peers]
    arrive(x_copies)
    x_core = send(xall.at[c], xall.at[c], other)
    arrive(a_copies)
    a_copies = ring(first_half, 3)
    arrive(b_copies)
    b_copies = [
        send(column(lax.rem(y + 1, NY), 2, 1), column(lax.rem(y + 1, NY), 2, 1), at_y(lax.rem(y + NY - 1, NY))),
        send(column(lax.rem(y + NY - 1, NY), 3, 1), column(lax.rem(y + NY - 1, NY), 3, 1), at_y(lax.rem(y + 1, NY))),
    ]
    inverse = eliminate(work, 40, RANK)[:, RANK:]
    ih = inverse.astype(bf16)
    il = (inverse - ih.astype(f32)).astype(bf16)
    inverse3 = jnp.concatenate([ih, ih, il], axis=1)

    def times_inverse(a):
        hi = a.astype(bf16)
        lo = (a - hi.astype(f32)).astype(bf16)
        return nn(inverse3, jnp.concatenate([hi, lo, hi], axis=0))

    xph[x, c] = times_inverse(both)
    token_copies = [send(xph.at[x, c], xph.at[x, c], at_xc(k, core)) for k, core in xc_peers]
    arrive(copies)
    total = zz[0]
    for k in range(1, NZ):
        total = total + zz[k]
    z3[:, y] = total
    copies = [send(z3.at[:, y], z3.at[:, y], at_y(k)) for k in y_peers]

    b, bv = b_ref[...], bv_ref[...]
    nb = jnp.sqrt(jnp.sum(b * b, keepdims=True))
    ng = jnp.zeros((1, 1), f32)
    for k in range(NX):
        gb = sums_ref[k, 0:6, :] * (1.0 / (256 * 64))
        ng = ng + jnp.sum(gb * gb, keepdims=True)
    ng = jnp.sqrt(ng)
    lane = lax.broadcasted_iota(jnp.int32, (1, flags_ref.shape[1]), 1)

    def skips(index):
        return jnp.sum(jnp.where(lane == index, flags_ref[...], 0), keepdims=True) == 1

    rb = jnp.where(skips(groups), 1.0, trust_coef * nb / (ng + decay_coef * nb))
    db = jnp.where(skips(groups), 0.0, decay_coef)
    biases = []
    for j in range(CB // HEAD):
        cols = pl.ds(pl.multiple_of(x * FEAT + c * CB + j * HEAD, HEAD), HEAD)
        gb = sums_ref[x, pl.ds(c * (CB // HEAD) + j, 1), :] * (1.0 / (256 * 64))
        biases.append(b_ref[:, cols] - momentum_coef * bv_ref[:, cols] - learn_rate * rb * (gb + db * b_ref[:, cols]))

    arrive(b_copies + [x_core])
    products(2, True)
    arrive(copies)
    for h in range(2):
        for k in range(4):
            zfull[c, h, x, :, k * QUART : (k + 1) * QUART] = z3[h, k]
    copies = [send(zfull.at[c, :, x], zfull.at[c, :, x], at_x(k)) for k in x_peers]
    products(3, False)
    arrive(a_copies)
    products(0, False)
    arrive(copies)
    copies = [send(zfull.at[c], zfull.at[c], other)]
    products(1, False)
    arrive(token_copies)
    for core in range(NC):
        for k in range(NX):
            part = xph[k, core].T[64:128]
            high = part.astype(bf16).astype(f32)
            tokens[core, k * 64 : (k + 1) * 64] = jnp.concatenate(
                [high, part - high, high, jnp.zeros_like(part)], axis=1
            ).astype(bf16)
    arrive(copies)

    cols = pl.ds(pl.multiple_of(lax.rem(x, 2) * FEAT + c * CB, 128), CB)
    zt = jnp.concatenate([zfull[core, x // 2, :, :, cols].reshape(32, CB) for core in range(NC)], axis=0)
    qc = times_inverse(zt) * (1.0 / (NC * NY * NZ))
    qh = qc.astype(bf16)
    ql = (qc - qh.astype(f32)).astype(bf16)
    right = jnp.concatenate([qh, qh, ql, jnp.zeros_like(qh)], axis=0)
    norms = sums_ref[0, 6:7] + sums_ref[1, 6:7] + sums_ref[2, 6:7] + sums_ref[3, 6:7]
    lanes = lax.broadcasted_iota(jnp.int32, (1, 128), 1)
    rates, decays = [], []
    for j in range(CB // HEAD):
        head = x * (FEAT // HEAD) + c * (CB // HEAD) + j
        part = qc[:, j * HEAD : (j + 1) * HEAD]
        nw = jnp.sqrt(jnp.sum(jnp.where(lanes == head, norms, 0.0), keepdims=True))
        na = jnp.sqrt(jnp.sum(part * part, keepdims=True))
        skip = skips(head)
        rates.append(learn_rate * jnp.where(skip, 1.0, trust_coef * nw / (na + decay_coef * nw)))
        decays.append(jnp.where(skip, 0.0, decay_coef))
    out_copies = []
    for core in (1 - c, c):
        moved[...] = nn(tokens[core], right)
        for j in range(CB // HEAD):
            cols = slice(j * HEAD, (j + 1) * HEAD)
            a = ya[core, :, cols]
            value = a + yb[core, :, cols] - rates[j] * (moved[:, cols] + decays[j] * a) + biases[j]
            for k in range(NX):
                osend[k, core, :, cols] = value[k * 64 : (k + 1) * 64].astype(bf16)
        for k in x_peers:
            out_copies.append(send(osend.at[k, core], orecv.at[x, c], at_xc(k, core)))
    out_copies.append(send(osend.at[x, 1 - c], orecv.at[x, c], other))
    orecv[x, c] = osend[x, c]

    for h in range(2):
        zt = jnp.concatenate([zfull[0, h].reshape(32, HALF), zfull[1, h].reshape(32, HALF)], axis=0)
        qt_ref[:, h * HALF : (h + 1) * HALF] = times_inverse(zt) * (1.0 / (NC * NY * NZ))
    left_ref[:, 0:256] = (x_ref[...].astype(f32) * (1.0 / 256)).T.astype(bf16)
    hat = times_inverse(pt)
    high = hat.astype(bf16).astype(f32)
    left_ref[:, 256:512] = jnp.concatenate([-high, high - hat, -high, jnp.zeros_like(hat)], axis=0).T.astype(bf16)
    feature = lax.broadcasted_iota(jnp.int32, (FEAT, 128), 0)
    wanted = lax.broadcasted_iota(jnp.int32, (FEAT, 128), 1)
    pick = jnp.where((feature == dp * own + wanted) & (wanted < own), 1.0, 0.0).astype(f32)
    own_ref[...] = jnp.dot(hat, pick, precision=lax.Precision.HIGHEST, preferred_element_type=f32)
    arrive(out_copies)
    for k in range(NX):
        for core in range(NC):
            out_ref[:, k * FEAT + core * CB : k * FEAT + core * CB + CB] = orecv[k, core]
    for copy in sent:
        copy.wait_send()


def step_call(x, g, e, factor, w, v, b, bv, flags):
    f32, bf16 = jnp.float32, jnp.bfloat16
    copies = 128
    return pl.pallas_call(
        step_kernel,
        out_shape=(
            jax.ShapeDtypeStruct((RANK, COLS), f32),
            jax.ShapeDtypeStruct((FEAT, 512), bf16),
            jax.ShapeDtypeStruct((NX, 8, 128), f32),
            jax.ShapeDtypeStruct((RANK, 128), f32),
            jax.ShapeDtypeStruct((64, COLS), bf16),
        ),
        in_specs=[pl.BlockSpec(memory_space=pltpu.VMEM)] * 2
        + [pl.BlockSpec(memory_space=pl.ANY)]
        + [pl.BlockSpec(memory_space=pltpu.VMEM)] * 6,
        out_specs=[pl.BlockSpec(memory_space=pltpu.VMEM)] * 5,
        scratch_shapes=[
            pltpu.VMEM((8, 8, PW), f32),
            pltpu.VMEM((8, 8, PW), f32),
            pltpu.VMEM((NZ, 8, PW), f32),
            pltpu.VMEM((8, 8, PW), f32),
            pltpu.VMEM((NX, RANK + 8, 128), f32),
            pltpu.VMEM((NX, RANK + 8, 128), f32),
            pltpu.VMEM((RANK, COLS), f32),
            pltpu.VMEM((32, COLS), f32),
            pltpu.VMEM((2, 4, 8, HALF), f32),
            pltpu.VMEM((2, 4, 8, HALF), f32),
            pltpu.VMEM((2, 4, 8, QUART), f32),
            pltpu.VMEM((2, 4, 8, QUART), f32),
            pltpu.VMEM((NZ, 2, 8, QUART), f32),
            pltpu.VMEM((2, 4, 8, QUART), f32),
            pltpu.VMEM((2, 2, 4, 8, HALF), f32),
            pltpu.VMEM((24, COLS), f32),
            pltpu.VMEM((NX, NC, 24, CB), f32),
            pltpu.VMEM((2, 24, CB), f32),
            pltpu.VMEM((NZ, NY, NX, 48, CB), bf16),
            pltpu.VMEM((NC, NX, 256, FEAT), bf16),
            pltpu.VMEM((FEAT, CB), bf16),
            pltpu.VMEM((FEAT, CB), bf16),
            pltpu.VMEM((NC, 256, CB), f32),
            pltpu.VMEM((NC, 256, CB), f32),
            pltpu.VMEM((NX, NC, RANK, 128), f32),
            pltpu.VMEM((NC, 256, 256), bf16),
            pltpu.VMEM((256, CB), f32),
            pltpu.VMEM((NX, NC, 64, CB), bf16),
            pltpu.VMEM((NX, NC, 64, CB), bf16),
            pltpu.VMEM((FEAT, COLS), bf16),
            pltpu.VMEM((8, 128), f32),
            pltpu.VMEM((COLS // HEAD, 128), f32),
            pltpu.SemaphoreType.DMA((LOADS,)),
            pltpu.SemaphoreType.DMA((copies,)),
            pltpu.SemaphoreType.DMA((copies,)),
        ],
        compiler_params=pltpu.CompilerParams(
            collective_id=0, has_side_effects=True, vmem_limit_bytes=56 * 2**20
        ),
        name="step",
    )(x, g, e, factor, w, v, b, bv, flags)


def finish_kernel(
    flags_ref, left_ref, g_ref, e_ref, qt_ref, sums_ref, own_ref, next_ref, w_ref, v_ref, b_ref, bv_ref,
    error_ref, weight_ref, velocity_ref, bias_ref, bias_velocity_ref, factor_ref, out_ref,
):
    f32, bf16 = jnp.float32, jnp.bfloat16
    highest = lax.Precision.HIGHEST
    step = pl.program_id(0)
    groups = COLS // HEAD

    @pl.when(step == 0)
    def _():
        total = jnp.concatenate(
            [sums_ref[k, r : r + 1, :] for k in range(NX) for r in range(FEAT // 128)], axis=1
        )
        gb = total * (1.0 / (256 * 64))
        b = b_ref[...]
        nb = jnp.sqrt(jnp.sum(b * b, keepdims=True))
        ng = jnp.sqrt(jnp.sum(gb * gb, keepdims=True))
        skip = flags_ref[groups] == 1
        rb = jnp.where(skip, 1.0, trust_coef * nb / (ng + decay_coef * nb))
        db = jnp.where(skip, 0.0, decay_coef)
        bv = momentum_coef * bv_ref[...] + learn_rate * rb * (gb + db * b)
        bias_velocity_ref[...] = bv
        bias_ref[...] = b - bv

    q = qt_ref[...]
    hi = q.astype(bf16)
    lo = (q - hi.astype(f32)).astype(bf16)
    right = jnp.concatenate([g_ref[...], hi, hi, lo, jnp.zeros_like(hi)], axis=0)
    error_ref[...] = (nn(left_ref[...], right) + e_ref[...].astype(f32)).astype(bf16)
    factor_ref[...] = hi
    out_ref[...] = next_ref[...]

    both = lax.dot_general(
        own_ref[...], q, (((0,), (0,)), ((), ())), precision=highest, preferred_element_type=f32
    )
    own = w_ref.shape[0]
    norms = sums_ref[0, 6:7] + sums_ref[1, 6:7] + sums_ref[2, 6:7] + sums_ref[3, 6:7]
    lane = lax.broadcasted_iota(jnp.int32, (1, 128), 1)
    per = TILE // HEAD
    for j in range(per):
        cols = slice(j * HEAD, (j + 1) * HEAD)
        head = step * per + j
        nw = jnp.sqrt(jnp.sum(jnp.where(lane == head, norms, 0.0), keepdims=True))
        na = jnp.sqrt(jnp.sum(q[:, cols] * q[:, cols], keepdims=True))
        skip = flags_ref[head] == 1
        rate = jnp.where(skip, 1.0, trust_coef * nw / (na + decay_coef * nw))
        decay = jnp.where(skip, 0.0, decay_coef)
        w = w_ref[:, 0, cols]
        v = momentum_coef * v_ref[:, 0, cols] + learn_rate * rate * (both[0:own, cols] + decay * w)
        velocity_ref[:, 0, cols] = v
        weight_ref[:, 0, cols] = w - v


def finish_call(flags, left, g, e, qt, sums, own, out, w, v, b, bv):
    f32, bf16 = jnp.float32, jnp.bfloat16

    def whole(a):
        return pl.BlockSpec(a.shape, lambda i: (0,) * a.ndim)

    def tiled(a):
        return pl.BlockSpec(a.shape[:-1] + (TILE,), lambda i: (0,) * (a.ndim - 1) + (i,))

    return pl.pallas_call(
        finish_kernel,
        grid=(COLS // TILE,),
        out_shape=(
            jax.ShapeDtypeStruct(e.shape, bf16),
            jax.ShapeDtypeStruct(w.shape, f32),
            jax.ShapeDtypeStruct(v.shape, f32),
            jax.ShapeDtypeStruct(b.shape, f32),
            jax.ShapeDtypeStruct(bv.shape, f32),
            jax.ShapeDtypeStruct((RANK, COLS), bf16),
            jax.ShapeDtypeStruct(out.shape, bf16),
        ),
        in_specs=[
            pl.BlockSpec(memory_space=pltpu.SMEM),
            whole(left), tiled(g), tiled(e), tiled(qt), whole(sums), whole(own), tiled(out),
            tiled(w), tiled(v), whole(b), whole(bv),
        ],
        out_specs=(
            tiled(e), tiled(w), tiled(v), whole(b), whole(bv),
            tiled(qt), tiled(out),
        ),
        compiler_params=pltpu.CompilerParams(vmem_limit_bytes=60 * 2**20),
        name="finish",
    )(flags, left, g, e, qt, sums, own, out, w, v, b, bv)


def shards(inputs, out_grads, error, weight, velocity, bias, bias_velocity, start_factor, flags):
    w, v = weight.transpose(1, 0, 2), velocity.transpose(1, 0, 2)
    b, bv = bias.reshape(1, COLS), bias_velocity.reshape(1, COLS)
    qt, left, sums, own, out = step_call(
        inputs, out_grads, error[0], start_factor.T, w, v, b, bv, flags.reshape(1, flags.shape[0])
    )
    error_new, weight_new, velocity_new, bias_new, bias_velocity_new, factor_new, next_out = finish_call(
        flags, left, out_grads, error[0], qt, sums, own, out, w, v, b, bv
    )
    return (
        error_new[None],
        weight_new.transpose(1, 0, 2),
        velocity_new.transpose(1, 0, 2),
        bias_new.reshape(COLS),
        bias_velocity_new.reshape(COLS),
        factor_new.T,
        next_out,
    )


def solution(mesh):
    in_specs = (
        P("dp", "fsdp"),
        P("dp", None),
        P("dp", "fsdp", None),
        P("fsdp", "dp", None),
        P("fsdp", "dp", None),
        P(),
        P(),
        P(),
        P(),
    )
    out_specs = (
        P("dp", "fsdp", None),
        P("fsdp", "dp", None),
        P("fsdp", "dp", None),
        P(),
        P(),
        P(),
        P(("dp", "fsdp"), None),
    )
    return jax.shard_map(shards, mesh=mesh, in_specs=in_specs, out_specs=out_specs, check_vma=False)
```
